256 devices in a mesh: segment: 8 (over y, core), shard: 32 (over x, z).
Axes of the slice: x: 4, y: 4, z: 8, core: 2. Of those that a mesh axis runs over, the one named last changes fastest.
Arguments:
- features: bfloat16 [8192, 512], P('shard'), may hold values from -6 to 6
- history: bfloat16 [16, 8192, 512], P('segment', 'shard'), may hold values from -6 to 6
- weight_self: bfloat16 [16, 512, 512], P('segment'), may hold values from -0.25 to 0.25
- weight_neigh: bfloat16 [16, 512, 512], P('segment'), may hold values from -0.25 to 0.25
- depth: int32 [8], P('segment'), may hold values from 1 to 2, as said below
- send_index: int32 [32, 32, 16], P('shard'), may hold values from 0 to 255
- pair_count: int32 [32, 32], replicated, may hold values from 1 to 16, as said below
- neighbours: int32 [8192, 16], P('shard'), may hold values from 0 to 767
- cotangent: bfloat16 [8192, 512], P('shard'), may hold values from -0.0625 to 0.0625
Outputs:
- new_history: bfloat16 [16, 8192, 512], P('segment', 'shard')
- grad_self: float32 [16, 512, 512], P('segment', 'shard')
- grad_neigh: float32 [16, 512, 512], P('segment', 'shard')
The draws below stay inside these ranges and needn't reach their ends.
Inputs may be any that keep to these rules, and one draw needn't show every extreme that they name: `depth`: some section has 2 active slots and some has 1. `pair_count`: each sending shard has a block with all 16 rows filled.
All inputs are finite; a program needn't handle non-finite values.
Results may differ from the reference program's by a relative error of at most 0.02.
Values may be sent and summed in bfloat16 or wider, within the bound.
No kernel may reach another device: no remote copies, remote signals or barrier semaphores. Data moves between devices by JAX's collectives and lax.ppermute only.
A program may use at most 64 MiB of HBM per device.

```python
import jax
import jax.numpy as jnp
from jax import lax

D = 512
FANOUT = 16
LMAX = 2
NODE_DEV = 256
ROWS_PAIR = 16
NODES = 8192
LAYERS = 16
N_SEGMENT = 8
N_SHARD = 32


def draw_depth(key, part):
    key = jax.random.fold_in(key, 11)
    segment_count = LAYERS // LMAX
    levels = jax.random.randint(key, (segment_count,), 1, LMAX + 1)
    shuffled = jax.random.permutation(jax.random.fold_in(key, 1), segment_count)
    position = jnp.arange(segment_count)
    levels = jnp.where(position == shuffled[0], LMAX, levels)
    levels = jnp.where(position == shuffled[1], 1, levels)
    return levels.astype(jnp.int32)


def draw_pair_count(key, part):
    key = jax.random.fold_in(key, 23)
    shard_count = NODES // NODE_DEV
    counts_drawn = jax.random.randint(key, (shard_count, shard_count), 1, ROWS_PAIR + 1)
    fullest = jax.random.randint(jax.random.fold_in(key, 1), (shard_count, 1), 0, shard_count)
    columns = jnp.arange(shard_count)[None, :]
    return jnp.where(columns == fullest, ROWS_PAIR, counts_drawn).astype(jnp.int32)


def with_ends(values, stream_key, low, largest):
    longest = values.shape.index(max(values.shape))
    spots = []
    for shift in (0, 1):
        where = [jax.random.randint(jax.random.fold_in(stream_key, axis), (), 0, length) for axis, length in enumerate(values.shape)]
        where[longest] = (where[longest] + shift) % values.shape[longest]
        spots.append(tuple(where))
    return values.at[spots[0]].set(low).at[spots[1]].set(largest)


def shard_levels(stream_key, shape, split, least, top_value):
    factor_of = 1.0
    for axis_at, shards_of in split:
        draws = jax.random.uniform(jax.random.fold_in(jax.random.fold_in(stream_key, 6), axis_at), (shards_of,), jnp.float32, least / len(split), top_value / len(split))
        factor_of = factor_of * jnp.repeat(jnp.exp(draws), shape[axis_at] // shards_of).reshape((-1,) + (1,) * (len(shape) - 1 - axis_at))
    return factor_of


def centred(key, dims, width, limit, split=(), kind=jnp.bfloat16):
    drawn = width * jax.random.normal(key, dims, jnp.float32)
    if split:
        drawn = drawn * shard_levels(key, dims, split, -0.22, 0.18)
    return jnp.clip(drawn, -limit, limit).astype(kind)


def setup_inputs(seed: int = 0) -> dict:
    keys = jax.random.split(jax.random.key(seed), 10)
    return {
        "features": centred(keys[0], (NODES, D), 1.0, 6.0, ((0, 32),)),
        "history": centred(keys[1], (LAYERS, NODES, D), 1.0, 6.0, ((0, 8), (1, 32))),
        "weight_self": centred(keys[2], (LAYERS, D, D), D ** -0.5, 0.25, ((0, 8),)),
        "weight_neigh": centred(keys[3], (LAYERS, D, D), D ** -0.5, 0.25, ((0, 8),)),
        "depth": draw_depth(jax.random.fold_in(keys[9], 71), 0),
        "send_index": with_ends(jax.random.randint(keys[5], (N_SHARD, N_SHARD, ROWS_PAIR), 0, NODE_DEV), jax.random.fold_in(keys[5], 1), 0, NODE_DEV - 1).astype(jnp.int32),
        "pair_count": draw_pair_count(jax.random.fold_in(keys[9], 71), 0),
        "neighbours": with_ends(jax.random.randint(keys[7], (NODES, FANOUT), 0, NODE_DEV + N_SHARD * ROWS_PAIR), jax.random.fold_in(keys[7], 1), 0, (NODE_DEV + N_SHARD * ROWS_PAIR) - 1).astype(jnp.int32),
        "cotangent": centred(keys[8], (NODES, D), NODES ** -0.5, 0.0625, ((0, 32),)),
    }


epsilon = 1e-06

def pre_activation(layer_in, mean_rows, self_weight, neigh_weight):
    return jnp.dot(layer_in, self_weight, preferred_element_type=jnp.float32) + jnp.dot(mean_rows, neigh_weight, preferred_element_type=jnp.float32)

def normalize(pre_norm):
    inverse = lax.rsqrt(lax.optimization_barrier(jnp.mean(pre_norm * pre_norm, axis=-1, keepdims=True)) + epsilon)
    return (inverse, pre_norm * inverse)

def layer_forward(layer_in, mean_rows, self_weight, neigh_weight):
    pre_norm = pre_activation(layer_in, mean_rows, self_weight, neigh_weight)
    inverse, normed = normalize(pre_norm)
    return (layer_in.astype(jnp.float32) + jax.nn.silu(normed)).astype(jnp.bfloat16)

def layer_backward(layer_in, mean_rows, pre_norm, self_weight, grad_out):
    inverse, normed = normalize(pre_norm)
    sigmoid = jax.nn.sigmoid(normed)
    grad_normed = grad_out.astype(jnp.float32) * sigmoid * (1.0 + normed * (1.0 - sigmoid))
    grad_pre = inverse * (grad_normed - normed * lax.optimization_barrier(jnp.mean(grad_normed * normed, axis=-1, keepdims=True)))
    grad_low = grad_pre.astype(jnp.bfloat16)
    back = lax.dot_general(grad_low, self_weight, (((1,), (1,)), ((), ())), preferred_element_type=jnp.float32)
    grad_in = (grad_out.astype(jnp.float32) + back).astype(jnp.bfloat16)
    self_term = lax.dot_general(layer_in, grad_low, (((0,), (0,)), ((), ())), preferred_element_type=jnp.float32)
    neigh_term = lax.dot_general(mean_rows, grad_low, (((0,), (0,)), ((), ())), preferred_element_type=jnp.float32)
    return (grad_in, self_term, neigh_term)

def reference(features, history, weight_self, weight_neigh, depth, send_index, pair_count, neighbours, cotangent):
    table_rows = NODE_DEV + N_SHARD * ROWS_PAIR
    live_slot = jnp.arange(ROWS_PAIR, dtype=jnp.int32)[None, None, :] < pair_count[:, :, None]
    source_rows = (jnp.arange(N_SHARD, dtype=jnp.int32) * NODE_DEV)[:, None, None] + send_index
    owner_base = (jnp.arange(NODES, dtype=jnp.int32) // NODE_DEV * table_rows)[:, None]
    table_index = (neighbours + owner_base).astype(jnp.int32)

    def aggregate(layer_history):
        sent = jnp.where(live_slot[..., None], layer_history[source_rows], jnp.zeros((), jnp.bfloat16))
        received = jnp.transpose(sent, (1, 0, 2, 3)).reshape(N_SHARD, N_SHARD * ROWS_PAIR, D)
        tables = jnp.concatenate([layer_history.reshape(N_SHARD, NODE_DEV, D), received], axis=1).reshape(N_SHARD * table_rows, D)

        def add_neighbour(neighbour_id, total):
            column = lax.dynamic_index_in_dim(table_index, neighbour_id, 1, keepdims=False)
            return total + tables[column].astype(jnp.float32)
        total = lax.fori_loop(0, FANOUT, add_neighbour, jnp.zeros((NODES, D), jnp.float32))
        return (total / FANOUT).astype(jnp.bfloat16)
    layer_input = features
    inputs_kept = []
    means_kept = []
    for segment_id in range(N_SEGMENT):
        for slot_id in range(LMAX):
            layer_id = segment_id * LMAX + slot_id
            active = slot_id < depth[segment_id]
            inputs_kept.append(layer_input)
            mean_rows = aggregate(history[layer_id])
            means_kept.append(mean_rows)
            result = layer_forward(layer_input, mean_rows, weight_self[layer_id], weight_neigh[layer_id])
            layer_input = jnp.where(active, result, layer_input)
    grad_rows = cotangent
    self_grads = [None] * LAYERS
    neigh_grads = [None] * LAYERS
    for layer_id in reversed(range(LAYERS)):
        segment_id, slot_id = divmod(layer_id, LMAX)
        active = slot_id < depth[segment_id]
        pre_norm = pre_activation(inputs_kept[layer_id], means_kept[layer_id], weight_self[layer_id], weight_neigh[layer_id])
        grad_in, self_term, neigh_term = layer_backward(inputs_kept[layer_id], means_kept[layer_id], pre_norm, weight_self[layer_id], grad_rows)
        grad_rows = jnp.where(active, grad_in, grad_rows)
        self_grads[layer_id] = jnp.where(active, self_term, jnp.zeros((), jnp.float32))
        neigh_grads[layer_id] = jnp.where(active, neigh_term, jnp.zeros((), jnp.float32))
    return (jnp.stack(inputs_kept), jnp.stack(self_grads), jnp.stack(neigh_grads))
```

```python
import functools

import jax
import jax.numpy as jnp
from jax import lax
from jax.experimental import pallas as pl
from jax.experimental.pallas import tpu as pltpu
from jax.sharding import Mesh
from jax.sharding import PartitionSpec as P

epsilon = 1e-06
SLOTS = 2
X_SIZE = 4
BF16 = jnp.bfloat16
F32 = jnp.float32
VMEM_LIMIT = 32 * 1024 * 1024


def matmul(a, b):
    return jnp.dot(a, b, preferred_element_type=F32)


def params(**extra):
    return pltpu.CompilerParams(vmem_limit_bytes=VMEM_LIMIT, **extra)


def whole(shape):
    zeros = (0,) * len(shape)
    return pl.BlockSpec(shape, lambda *_: zeros)


def pick_kernel(index_ref, history_ref, out_ref):
    slots, nodes, width = history_ref.shape
    shards, _, rows, _ = out_ref.shape
    columns = lax.broadcasted_iota(jnp.int32, (shards * rows, nodes), 1)
    chosen = (index_ref[...] == columns).astype(F32).astype(BF16)
    for slot in range(slots):
        picked = matmul(chosen, history_ref[slot]).astype(BF16)
        out_ref[:, slot] = picked.reshape(shards, rows, width)


def count_kernel(neighbours_ref, live_ref, history_ref, counts_ref, own_ref):
    slots, nodes, width = history_ref.shape
    fanout = neighbours_ref.shape[1]
    received = counts_ref.shape[1]
    table = nodes + received
    columns = lax.broadcasted_iota(jnp.int32, (nodes, table), 1)
    total = jnp.zeros((nodes, table), F32)
    for k in range(fanout):
        total += jnp.where(neighbours_ref[:, k : k + 1] == columns, 1.0, 0.0)
    counts_ref[...] = (total[:, nodes:] * live_ref[...]).astype(BF16)
    own = total[:, :nodes].astype(BF16)
    for slot in range(slots):
        own_ref[slot] = matmul(own, history_ref[slot])


def mean_kernel(depth_ref, counts_ref, own_ref, received_ref, weight_ref, mean_ref, term_ref, *, fanout):
    slots, nodes, width = own_ref.shape
    segments = term_ref.shape[0]
    part = nodes // segments
    for slot in range(slots):
        rows = received_ref[:, slot].reshape(-1, width)
        total = own_ref[slot] + matmul(counts_ref[...], rows)
        mean = (total * (1.0 / fanout)).astype(BF16)
        mean_ref[slot] = mean
        term = matmul(mean, weight_ref[slot]).astype(BF16)
        term_ref[:, slot * part : (slot + 1) * part] = term.reshape(segments, part, width)
    flag = depth_ref[0].astype(F32)
    tail = term_ref.shape[1] - slots * part
    term_ref[:, slots * part :] = jnp.full((segments, tail, width), flag, F32).astype(BF16)


def is_active(flag, layer):
    depth = jnp.max(flag.astype(F32))
    return (layer % SLOTS).astype(F32) + 0.5 < depth


def normalize(pre_norm):
    inverse = lax.rsqrt(jnp.mean(pre_norm * pre_norm, axis=-1, keepdims=True) + epsilon)
    return inverse, pre_norm * inverse


def forward_kernel(segment_ref, features_ref, weight_ref, term_ref, flag_ref, x_ref, pre_ref, state):
    layer = pl.program_id(0)

    @pl.when(layer == 0)
    def _():
        state[...] = features_ref[...]

    x = state[...]
    x_ref[0, :, 0] = jnp.broadcast_to(x[None], (x_ref.shape[1],) + x.shape)

    @pl.when(is_active(flag_ref[0], layer))
    def _():
        pre_norm = matmul(x, weight_ref[0]) + term_ref[0].astype(F32)
        pre_ref[0] = pre_norm
        _, normed = normalize(pre_norm)
        state[...] = (x.astype(F32) + normed * jax.nn.sigmoid(normed)).astype(BF16)


def backward_kernel(segment_ref, cotangent_ref, weight_ref, pre_ref, flag_ref, out_ref, state):
    step = pl.program_id(0)
    layer = pl.num_programs(0) - 1 - step
    parts = out_ref.shape[1]
    columns = out_ref.shape[4]

    @pl.when(step == 0)
    def _():
        state[...] = cotangent_ref[...]

    active = is_active(flag_ref[0], layer)

    @pl.when(active)
    def _():
        inverse, normed = normalize(pre_ref[0])
        grad_out = state[...].astype(F32)
        sigmoid = jax.nn.sigmoid(normed)
        grad_normed = grad_out * sigmoid * (1.0 + normed * (1.0 - sigmoid))
        grad_pre = inverse * (
            grad_normed - normed * jnp.mean(grad_normed * normed, axis=-1, keepdims=True)
        )
        low = grad_pre.astype(BF16)
        for part in range(parts):
            out_ref[0, part, 0] = low[:, part * columns : (part + 1) * columns]
        back = lax.dot_general(
            low, weight_ref[0], (((1,), (1,)), ((), ())), preferred_element_type=F32
        )
        state[...] = (grad_out + back).astype(BF16)

    @pl.when(jnp.logical_not(active))
    def _():
        out_ref[...] = jnp.zeros_like(out_ref)


def product_kernel(x_ref, mean_ref, grad_ref, out_ref):
    segments, parts, slots, rows, width = x_ref.shape
    columns = grad_ref.shape[4]
    shards, _, _, out_rows, _ = out_ref.shape
    for slot in range(slots):
        sums = [None, None]
        for part in range(parts):
            grad = grad_ref[:, part, slot].reshape(segments * rows, columns)
            layer_in = x_ref[:, part, slot].reshape(segments * rows, width)
            for kind, left in enumerate((layer_in, mean_ref[part, slot])):
                term = lax.dot_general(
                    grad, left, (((0,), (0,)), ((), ())), preferred_element_type=F32
                )
                sums[kind] = term if sums[kind] is None else sums[kind] + term
        for kind in range(2):
            result = sums[kind].T.astype(BF16)
            out_ref[:, kind, slot] = result.reshape(shards, out_rows, columns)


def sum_kernel(parts_ref, self_ref, neigh_ref):
    slots, rows, width = self_ref.shape
    columns = parts_ref.shape[5]
    for part in range(parts_ref.shape[0]):
        total = jnp.sum(parts_ref[part].astype(F32), axis=0)
        self_ref[:, :, part * columns : (part + 1) * columns] = total[0]
        neigh_ref[:, :, part * columns : (part + 1) * columns] = total[1]


def history_kernel(mine_ref, x_ref, out_ref):
    segments, _, slots, rows, width = x_ref.shape
    for slot in range(slots):
        out_ref[slot] = x_ref[:, 0, slot].reshape(segments * rows, width)


def exchange(block, axes):
    return lax.all_to_all(block, axes, split_axis=0, concat_axis=0, tiled=True)


def body(
    features,
    history,
    weight_self,
    weight_neigh,
    depth,
    send_index,
    pair_count,
    neighbours,
    cotangent,
):
    segments = lax.axis_size("segment")
    x_size = lax.axis_size("x")
    z_size = lax.axis_size("z")
    shards = x_size * z_size
    my_segment = lax.axis_index("segment").reshape(1)
    my_x = lax.axis_index("x").reshape(1)
    my_shard = lax.axis_index(("x", "z"))
    slots, nodes, width = history.shape
    rows_pair = send_index.shape[2]
    fanout = neighbours.shape[1]
    layers = segments * slots
    part = nodes // segments
    columns = width // x_size
    received_rows = shards * rows_pair

    all_self = lax.all_gather(weight_self, "segment", axis=0, tiled=True)

    outgoing = pl.pallas_call(
        pick_kernel,
        out_shape=jax.ShapeDtypeStruct((shards, slots, rows_pair, width), BF16),
        compiler_params=params(),
        name="pick_rows",
    )(send_index.reshape(received_rows, 1), history)
    received = exchange(outgoing, ("x", "z"))

    my_counts = lax.dynamic_index_in_dim(pair_count, my_shard, 1, keepdims=True)
    live = (lax.iota(jnp.int32, rows_pair)[None, :] < my_counts).astype(F32)
    counts, own = pl.pallas_call(
        count_kernel,
        out_shape=(
            jax.ShapeDtypeStruct((nodes, received_rows), BF16),
            jax.ShapeDtypeStruct((slots, nodes, width), F32),
        ),
        compiler_params=params(),
        cost_estimate=pl.CostEstimate(
            flops=2 * slots * nodes * nodes * width, bytes_accessed=6 << 20, transcendentals=0
        ),
        name="count_rows",
    )(neighbours, live.reshape(1, received_rows), history)

    term_rows = slots * part + 16
    mean, terms = pl.pallas_call(
        functools.partial(mean_kernel, fanout=fanout),
        in_specs=[pl.BlockSpec(memory_space=pltpu.SMEM)]
        + [pl.BlockSpec(memory_space=pltpu.VMEM)] * 4,
        out_shape=(
            jax.ShapeDtypeStruct((slots, nodes, width), BF16),
            jax.ShapeDtypeStruct((segments, term_rows, width), BF16),
        ),
        compiler_params=params(),
        name="neighbour_mean",
    )(depth, counts, own, received, weight_neigh)
    all_mean = lax.all_gather(mean, "x", axis=0, tiled=False)
    all_terms = exchange(terms, "segment")

    sequential = pltpu.CompilerParams(
        dimension_semantics=("arbitrary",), vmem_limit_bytes=VMEM_LIMIT
    )
    layer_flops = 2 * layers * part * width * width
    x_all, pre_all = pl.pallas_call(
        forward_kernel,
        grid_spec=pltpu.PrefetchScalarGridSpec(
            num_scalar_prefetch=1,
            grid=(layers,),
            in_specs=[
                pl.BlockSpec((part, width), lambda i, s: (s[0], 0)),
                pl.BlockSpec((1, width, width), lambda i, s: (i, 0, 0)),
                pl.BlockSpec((1, part, width), lambda i, s: (i // SLOTS, i % SLOTS, 0)),
                pl.BlockSpec((1, 16, width), lambda i, s: (i // SLOTS, slots * part // 16, 0)),
            ],
            out_specs=[
                pl.BlockSpec(
                    (1, x_size, 1, part, width), lambda i, s: (i // SLOTS, 0, i % SLOTS, 0, 0)
                ),
                pl.BlockSpec((1, part, width), lambda i, s: (i, 0, 0)),
            ],
            scratch_shapes=[pltpu.VMEM((part, width), BF16)],
        ),
        out_shape=(
            jax.ShapeDtypeStruct((segments, x_size, slots, part, width), BF16),
            jax.ShapeDtypeStruct((layers, part, width), F32),
        ),
        compiler_params=sequential,
        cost_estimate=pl.CostEstimate(
            flops=layer_flops, bytes_accessed=12 << 20, transcendentals=layers * part * width
        ),
        name="forward_layers",
    )(my_segment, features, all_self, all_terms, all_terms)
    x_parts = exchange(x_all.reshape(segments * x_size, slots, part, width), ("segment", "x"))
    x_parts = x_parts.reshape(segments, x_size, slots, part, width)

    last = layers - 1
    grad_all = pl.pallas_call(
        backward_kernel,
        grid_spec=pltpu.PrefetchScalarGridSpec(
            num_scalar_prefetch=1,
            grid=(layers,),
            in_specs=[
                pl.BlockSpec((part, width), lambda i, s: (s[0], 0)),
                pl.BlockSpec((1, width, width), lambda i, s: (last - i, 0, 0)),
                pl.BlockSpec((1, part, width), lambda i, s: (last - i, 0, 0)),
                pl.BlockSpec(
                    (1, 16, width), lambda i, s: ((last - i) // SLOTS, slots * part // 16, 0)
                ),
            ],
            out_specs=pl.BlockSpec(
                (1, x_size, 1, part, columns),
                lambda i, s: ((last - i) // SLOTS, 0, (last - i) % SLOTS, 0, 0),
            ),
            scratch_shapes=[pltpu.VMEM((part, width), BF16)],
        ),
        out_shape=jax.ShapeDtypeStruct((segments, x_size, slots, part, columns), BF16),
        compiler_params=sequential,
        cost_estimate=pl.CostEstimate(
            flops=layer_flops, bytes_accessed=12 << 20, transcendentals=layers * part * width
        ),
        name="backward_layers",
    )(my_segment, cotangent, all_self, pre_all, all_terms)
    grad_parts = exchange(grad_all.reshape(segments * x_size, slots, part, columns), ("segment", "x"))
    grad_parts = grad_parts.reshape(segments, x_size, slots, part, columns)

    out_rows = width // shards
    products = pl.pallas_call(
        product_kernel,
        out_shape=jax.ShapeDtypeStruct((shards, 2, slots, out_rows, columns), BF16),
        compiler_params=params(),
        name="weight_products",
    )(x_parts, all_mean, grad_parts)
    summands = exchange(products, ("x", "z"))
    grad_shape = jax.ShapeDtypeStruct((slots, out_rows, width), F32)
    grad_self, grad_neigh = pl.pallas_call(
        sum_kernel,
        out_shape=(grad_shape, grad_shape),
        compiler_params=params(),
        name="sum_products",
    )(summands.reshape(x_size, z_size, 2, slots, out_rows, columns))

    new_history = pl.pallas_call(
        history_kernel,
        grid_spec=pltpu.PrefetchScalarGridSpec(
            num_scalar_prefetch=1,
            grid=(1,),
            in_specs=[
                pl.BlockSpec(
                    (segments, 1, slots, part, width), lambda i, s: (0, s[0], 0, 0, 0)
                )
            ],
            out_specs=pl.BlockSpec((slots, nodes, width), lambda i, s: (0, 0, 0)),
        ),
        out_shape=jax.ShapeDtypeStruct((slots, nodes, width), BF16),
        compiler_params=params(),
        cost_estimate=pl.CostEstimate(flops=0, bytes_accessed=1 << 20, transcendentals=0),
        name="new_history",
    )(my_x, x_parts)
    return (new_history, grad_self, grad_neigh)


def solution(mesh):
    segments, shards = mesh.devices.shape
    split = Mesh(
        mesh.devices.reshape(segments, X_SIZE, shards // X_SIZE), ("segment", "x", "z")
    )
    shard = ("x", "z")
    return jax.shard_map(
        body,
        mesh=split,
        in_specs=(
            P(shard, None),
            P("segment", shard, None),
            P("segment", None, None),
            P("segment", None, None),
            P("segment"),
            P(shard, None, None),
            P(),
            P(shard, None),
            P(shard, None),
        ),
        out_specs=(
            P("segment", shard, None),
            P("segment", shard, None),
            P("segment", shard, None),
        ),
        check_vma=False,
    )
```

```python
import functools

import jax
import jax.numpy as jnp
from jax import lax
from jax.experimental import pallas as pl
from jax.experimental.pallas import tpu as pltpu
from jax.sharding import Mesh
from jax.sharding import PartitionSpec as P

epsilon = 1e-06
SLOTS = 2
X_SIZE = 4
BF16 = jnp.bfloat16
F32 = jnp.float32
VMEM_LIMIT = 32 * 1024 * 1024


def matmul(a, b):
    return jnp.dot(a, b, preferred_element_type=F32)


def params(**extra):
    return pltpu.CompilerParams(vmem_limit_bytes=VMEM_LIMIT, **extra)


def whole(shape):
    zeros = (0,) * len(shape)
    return pl.BlockSpec(shape, lambda *_: zeros)


def pick_kernel(index_ref, history_ref, out_ref):
    slots, nodes, width = history_ref.shape
    shards, _, rows, _ = out_ref.shape
    columns = lax.broadcasted_iota(jnp.int32, (shards * rows, nodes), 1)
    chosen = (index_ref[...] == columns).astype(F32).astype(BF16)
    for slot in range(slots):
        picked = matmul(chosen, history_ref[slot]).astype(BF16)
        out_ref[:, slot] = picked.reshape(shards, rows, width)


def count_kernel(neighbours_ref, live_ref, history_ref, counts_ref, own_ref):
    slots, nodes, width = history_ref.shape
    fanout = neighbours_ref.shape[1]
    received = counts_ref.shape[1]
    table = nodes + received
    columns = lax.broadcasted_iota(jnp.int32, (nodes, table), 1)
    total = jnp.zeros((nodes, table), F32)
    for k in range(fanout):
        total += jnp.where(neighbours_ref[:, k : k + 1] == columns, 1.0, 0.0)
    counts_ref[...] = (total[:, nodes:] * live_ref[...]).astype(BF16)
    own = total[:, :nodes].astype(BF16)
    for slot in range(slots):
        own_ref[slot] = matmul(own, history_ref[slot])


def mean_kernel(depth_ref, counts_ref, own_ref, received_ref, weight_ref, mean_ref, term_ref, *, fanout):
    slots, nodes, width = own_ref.shape
    segments = term_ref.shape[0]
    part = nodes // segments
    for slot in range(slots):
        rows = received_ref[:, slot].reshape(-1, width)
        total = own_ref[slot] + matmul(counts_ref[...], rows)
        mean = (total * (1.0 / fanout)).astype(BF16)
        mean_ref[slot] = mean
        term = matmul(mean, weight_ref[slot]).astype(BF16)
        term_ref[:, slot * part : (slot + 1) * part] = term.reshape(segments, part, width)
    flag = depth_ref[0].astype(F32)
    tail = term_ref.shape[1] - slots * part
    term_ref[:, slots * part :] = jnp.full((segments, tail, width), flag, F32).astype(BF16)


def is_active(flag, layer):
    depth = jnp.max(flag.astype(F32))
    return (layer % SLOTS).astype(F32) + 0.5 < depth


def normalize(pre_norm):
    inverse = lax.rsqrt(jnp.mean(pre_norm * pre_norm, axis=-1, keepdims=True) + epsilon)
    return inverse, pre_norm * inverse


def forward_kernel(segment_ref, features_ref, weight_ref, term_ref, flag_ref, x_ref, pre_ref, state):
    layer = pl.program_id(0)

    @pl.when(layer == 0)
    def _():
        state[...] = features_ref[...]

    x = state[...]
    x_ref[0, 0] = x

    @pl.when(is_active(flag_ref[0], layer))
    def _():
        pre_norm = matmul(x, weight_ref[0]) + term_ref[0].astype(F32)
        pre_ref[0] = pre_norm
        _, normed = normalize(pre_norm)
        state[...] = (x.astype(F32) + normed * jax.nn.sigmoid(normed)).astype(BF16)


def backward_kernel(segment_ref, cotangent_ref, weight_ref, pre_ref, flag_ref, out_ref, state):
    step = pl.program_id(0)
    layer = pl.num_programs(0) - 1 - step
    parts = out_ref.shape[1]
    columns = out_ref.shape[4]

    @pl.when(step == 0)
    def _():
        state[...] = cotangent_ref[...]

    active = is_active(flag_ref[0], layer)

    @pl.when(active)
    def _():
        inverse, normed = normalize(pre_ref[0])
        grad_out = state[...].astype(F32)
        sigmoid = jax.nn.sigmoid(normed)
        grad_normed = grad_out * sigmoid * (1.0 + normed * (1.0 - sigmoid))
        grad_pre = inverse * (
            grad_normed - normed * jnp.mean(grad_normed * normed, axis=-1, keepdims=True)
        )
        low = grad_pre.astype(BF16)
        for part in range(parts):
            out_ref[0, part, 0] = low[:, part * columns : (part + 1) * columns]
        back = lax.dot_general(
            low, weight_ref[0], (((1,), (1,)), ((), ())), preferred_element_type=F32
        )
        state[...] = (grad_out + back).astype(BF16)

    @pl.when(jnp.logical_not(active))
    def _():
        out_ref[...] = jnp.zeros_like(out_ref)


def product_kernel(
    place_ref, grad_ref, mean_own, mean_next, mean_far0, mean_far1, mean_last,
    x_own, x_next, x_far0, x_far1, x_last, out_ref,
):
    segments, parts, slots, rows, columns = grad_ref.shape
    shards, _, _, out_rows, _ = out_ref.shape
    half = segments // 2
    for slot in range(slots):
        self_sum = neigh_sum = None
        for ahead in range(parts):
            part = lax.rem(place_ref[0] + ahead, parts)
            grad = grad_ref[:, part, slot].reshape(segments * rows, columns)
            if ahead == 2:
                mean = (mean_far0, mean_far1)[slot][0]
                layer_in = jnp.concatenate(
                    [ref[:, slot].reshape(half * rows, -1) for ref in (x_far0, x_far1)], axis=0
                )
            else:
                mean = (mean_own, mean_next, None, mean_last)[ahead][slot]
                layer_in = (x_own, x_next, None, x_last)[ahead][:, slot].reshape(
                    segments * rows, -1
                )
            self_term, neigh_term = (
                lax.dot_general(grad, left, (((0,), (0,)), ((), ())), preferred_element_type=F32)
                for left in (layer_in, mean)
            )
            self_sum = self_term if self_sum is None else self_sum + self_term
            neigh_sum = neigh_term if neigh_sum is None else neigh_sum + neigh_term
        for kind, total in enumerate((self_sum, neigh_sum)):
            out_ref[:, kind, slot] = total.T.astype(BF16).reshape(shards, out_rows, columns)


def sum_kernel(parts_ref, self_ref, neigh_ref):
    slots, rows, width = self_ref.shape
    columns = parts_ref.shape[5]
    for part in range(parts_ref.shape[0]):
        total = jnp.sum(parts_ref[part].astype(F32), axis=0)
        self_ref[:, :, part * columns : (part + 1) * columns] = total[0]
        neigh_ref[:, :, part * columns : (part + 1) * columns] = total[1]


def history_kernel(x_ref, out_ref):
    segments, slots, rows, width = x_ref.shape
    for slot in range(slots):
        out_ref[slot] = x_ref[:, slot].reshape(segments * rows, width)


def shifted(block, axis, shift):
    size = lax.axis_size(axis)
    return lax.ppermute(block, axis, [(i, (i + shift) % size) for i in range(size)])


def ring_of_four(block, axis, step):
    half = block.shape[0] // 2
    last = shifted(block, axis, step)
    following = shifted(block, axis, -step)
    far0 = shifted(last[:half], axis, step)
    far1 = shifted(following[half:], axis, -step)
    return block, following, far0, far1, last


def core_swap(block):
    size = lax.axis_size("segment")
    return lax.ppermute(block, "segment", [(i, i ^ 1) for i in range(size)])


def exchange(block, axes):
    return lax.all_to_all(block, axes, split_axis=0, concat_axis=0, tiled=True)


def body(
    features,
    history,
    weight_self,
    weight_neigh,
    depth,
    send_index,
    pair_count,
    neighbours,
    cotangent,
):
    segments = lax.axis_size("segment")
    x_size = lax.axis_size("x")
    z_size = lax.axis_size("z")
    shards = x_size * z_size
    my_segment = lax.axis_index("segment").reshape(1)
    my_x = lax.axis_index("x").reshape(1)
    my_shard = lax.axis_index(("x", "z"))
    slots, nodes, width = history.shape
    rows_pair = send_index.shape[2]
    fanout = neighbours.shape[1]
    layers = segments * slots
    part = nodes // segments
    columns = width // x_size
    received_rows = shards * rows_pair

    pieces = []
    for piece in ring_of_four(weight_self, "segment", 2):
        pieces.append((piece, core_swap(piece)))
    own_w, next_w, far0_w, far1_w, last_w = pieces
    all_self = jnp.concatenate(
        [*own_w, *next_w, far0_w[0], far1_w[0], far0_w[1], far1_w[1], *last_w], axis=0
    )

    def place_of(layer, segment):
        section = layer // SLOTS
        ahead = lax.rem(section // 2 - segment // 2 + 4, 4)
        return (ahead * 2 + lax.rem(section + segment, 2)) * SLOTS + lax.rem(layer, SLOTS)

    outgoing = pl.pallas_call(
        pick_kernel,
        out_shape=jax.ShapeDtypeStruct((shards, slots, rows_pair, width), BF16),
        compiler_params=params(),
        name="pick_rows",
    )(send_index.reshape(received_rows, 1), history)
    received = exchange(outgoing, ("x", "z"))

    my_counts = lax.dynamic_index_in_dim(pair_count, my_shard, 1, keepdims=True)
    live = (lax.iota(jnp.int32, rows_pair)[None, :] < my_counts).astype(F32)
    counts, own = pl.pallas_call(
        count_kernel,
        out_shape=(
            jax.ShapeDtypeStruct((nodes, received_rows), BF16),
            jax.ShapeDtypeStruct((slots, nodes, width), F32),
        ),
        compiler_params=params(),
        cost_estimate=pl.CostEstimate(
            flops=2 * slots * nodes * nodes * width, bytes_accessed=6 << 20, transcendentals=0
        ),
        name="count_rows",
    )(neighbours, live.reshape(1, received_rows), history)

    term_rows = slots * part + 16
    mean, terms = pl.pallas_call(
        functools.partial(mean_kernel, fanout=fanout),
        in_specs=[pl.BlockSpec(memory_space=pltpu.SMEM)]
        + [pl.BlockSpec(memory_space=pltpu.VMEM)] * 4,
        out_shape=(
            jax.ShapeDtypeStruct((slots, nodes, width), BF16),
            jax.ShapeDtypeStruct((segments, term_rows, width), BF16),
        ),
        compiler_params=params(),
        name="neighbour_mean",
    )(depth, counts, own, received, weight_neigh)
    means = ring_of_four(mean, "x", 1)
    all_terms = exchange(terms, "segment")

    sequential = pltpu.CompilerParams(
        dimension_semantics=("arbitrary",), vmem_limit_bytes=VMEM_LIMIT
    )
    layer_flops = 2 * layers * part * width * width
    x_all, pre_all = pl.pallas_call(
        forward_kernel,
        grid_spec=pltpu.PrefetchScalarGridSpec(
            num_scalar_prefetch=1,
            grid=(layers,),
            in_specs=[
                pl.BlockSpec((part, width), lambda i, s: (s[0], 0)),
                pl.BlockSpec((1, width, width), lambda i, s: (place_of(i, s[0]), 0, 0)),
                pl.BlockSpec((1, part, width), lambda i, s: (i // SLOTS, i % SLOTS, 0)),
                pl.BlockSpec((1, 16, width), lambda i, s: (i // SLOTS, slots * part // 16, 0)),
            ],
            out_specs=[
                pl.BlockSpec((1, 1, part, width), lambda i, s: (i // SLOTS, i % SLOTS, 0, 0)),
                pl.BlockSpec((1, part, width), lambda i, s: (i, 0, 0)),
            ],
            scratch_shapes=[pltpu.VMEM((part, width), BF16)],
        ),
        out_shape=(
            jax.ShapeDtypeStruct((segments, slots, part, width), BF16),
            jax.ShapeDtypeStruct((layers, part, width), F32),
        ),
        compiler_params=sequential,
        cost_estimate=pl.CostEstimate(
            flops=layer_flops, bytes_accessed=12 << 20, transcendentals=layers * part * width
        ),
        name="forward_layers",
    )(my_segment, features, all_self, all_terms, all_terms)
    x_own = exchange(x_all, "segment")

    last = layers - 1
    grad_all = pl.pallas_call(
        backward_kernel,
        grid_spec=pltpu.PrefetchScalarGridSpec(
            num_scalar_prefetch=1,
            grid=(layers,),
            in_specs=[
                pl.BlockSpec((part, width), lambda i, s: (s[0], 0)),
                pl.BlockSpec((1, width, width), lambda i, s: (place_of(last - i, s[0]), 0, 0)),
                pl.BlockSpec((1, part, width), lambda i, s: (last - i, 0, 0)),
                pl.BlockSpec(
                    (1, 16, width), lambda i, s: ((last - i) // SLOTS, slots * part // 16, 0)
                ),
            ],
            out_specs=pl.BlockSpec(
                (1, x_size, 1, part, columns),
                lambda i, s: ((last - i) // SLOTS, 0, (last - i) % SLOTS, 0, 0),
            ),
            scratch_shapes=[pltpu.VMEM((part, width), BF16)],
        ),
        out_shape=jax.ShapeDtypeStruct((segments, x_size, slots, part, columns), BF16),
        compiler_params=sequential,
        cost_estimate=pl.CostEstimate(
            flops=layer_flops, bytes_accessed=12 << 20, transcendentals=layers * part * width
        ),
        name="backward_layers",
    )(my_segment, cotangent, all_self, pre_all, all_terms)
    grad_all, x_own, means = lax.optimization_barrier((grad_all, x_own, means))
    xs = ring_of_four(x_own, "x", 1)
    grad_parts = exchange(grad_all.reshape(segments * x_size, slots, part, columns), ("segment", "x"))
    grad_parts = grad_parts.reshape(segments, x_size, slots, part, columns)

    out_rows = width // shards
    products = pl.pallas_call(
        product_kernel,
        in_specs=[pl.BlockSpec(memory_space=pltpu.SMEM)]
        + [pl.BlockSpec(memory_space=pltpu.VMEM)] * 11,
        out_shape=jax.ShapeDtypeStruct((shards, 2, slots, out_rows, columns), BF16),
        compiler_params=params(),
        name="weight_products",
    )(my_x, grad_parts, *means, *xs)
    summands = exchange(products, ("x", "z"))
    grad_shape = jax.ShapeDtypeStruct((slots, out_rows, width), F32)
    grad_self, grad_neigh = pl.pallas_call(
        sum_kernel,
        out_shape=(grad_shape, grad_shape),
        compiler_params=params(),
        name="sum_products",
    )(summands.reshape(x_size, z_size, 2, slots, out_rows, columns))

    new_history = pl.pallas_call(
        history_kernel,
        out_shape=jax.ShapeDtypeStruct((slots, nodes, width), BF16),
        compiler_params=params(),
        cost_estimate=pl.CostEstimate(flops=0, bytes_accessed=1 << 20, transcendentals=0),
        name="new_history",
    )(x_own)
    return (new_history, grad_self, grad_neigh)


def solution(mesh):
    segments, shards = mesh.devices.shape
    split = Mesh(
        mesh.devices.reshape(segments, X_SIZE, shards // X_SIZE), ("segment", "x", "z")
    )
    shard = ("x", "z")
    return jax.shard_map(
        body,
        mesh=split,
        in_specs=(
            P(shard, None),
            P("segment", shard, None),
            P("segment", None, None),
            P("segment", None, None),
            P("segment"),
            P(shard, None, None),
            P(),
            P(shard, None),
            P(shard, None),
        ),
        out_specs=(
            P("segment", shard, None),
            P("segment", shard, None),
            P("segment", shard, None),
        ),
        check_vma=False,
    )
```

```python
import functools

import jax
import jax.numpy as jnp
from jax import lax
from jax.experimental import pallas as pl
from jax.experimental.pallas import tpu as pltpu
from jax.sharding import Mesh
from jax.sharding import PartitionSpec as P

epsilon = 1e-06
SLOTS = 2
PAIR = 2
BF16 = jnp.bfloat16
F32 = jnp.float32
MIB = 1024 * 1024


def matmul(a, b):
    return jnp.dot(a, b, preferred_element_type=F32)


def params(mib):
    return pltpu.CompilerParams(vmem_limit_bytes=int(mib * MIB))


def lasting(microseconds):
    return pl.CostEstimate(
        flops=int(microseconds * 1.15e9), bytes_accessed=4 * MIB, transcendentals=0
    )


def pick_kernel(index_ref, history_ref, out_ref):
    slots, nodes, width = history_ref.shape
    shards, _, rows, _ = out_ref.shape
    columns = lax.broadcasted_iota(jnp.int32, (shards * rows, nodes), 1)
    chosen = (index_ref[...] == columns).astype(F32).astype(BF16)
    for slot in range(slots):
        picked = matmul(chosen, history_ref[slot]).astype(BF16)
        out_ref[:, slot] = picked.reshape(shards, rows, width)


def token_kernel(in_ref, out_ref):
    out_ref[0, 0] = in_ref[0, 0]


def count_kernel(neighbours_ref, live_ref, out_ref, counts_ref, sem):
    nodes, table = counts_ref.shape
    columns = lax.broadcasted_iota(jnp.int32, (nodes, table), 1)
    total = jnp.zeros((nodes, table), F32)
    for k in range(neighbours_ref.shape[1]):
        total += jnp.where(neighbours_ref[:, k : k + 1] == columns, 1.0, 0.0)
    counts_ref[...] = (total * live_ref[...]).astype(BF16)
    copy = pltpu.make_async_copy(counts_ref, out_ref, sem)
    copy.start()
    copy.wait()


def mean_kernel(
    depth_ref, half_ref, received_ref, counts_hbm, history_hbm, weight_hbm,
    mine_hbm, others_hbm, term_hbm,
    counts_ref, history_ref, weight_ref, mine_ref, others_ref, term_ref, sems, *, fanout,
):
    slots, nodes, width = history_ref.shape
    segments = term_ref.shape[0]
    part = nodes // segments
    loads = [
        pltpu.make_async_copy(hbm, ref, sems.at[i])
        for i, (hbm, ref) in enumerate(
            ((counts_hbm, counts_ref), (history_hbm, history_ref), (weight_hbm, weight_ref))
        )
    ]
    for load in loads:
        load.start()
    flag = depth_ref[0].astype(F32)
    tail = term_ref.shape[1] - slots * part
    term_ref[:, slots * part :] = jnp.full((segments, tail, width), flag, F32).astype(BF16)
    loads[0].wait()
    far = [
        matmul(counts_ref[:, nodes:], received_ref[:, slot].reshape(-1, width))
        for slot in range(slots)
    ]
    loads[1].wait()
    means = [
        ((far[slot] + matmul(counts_ref[:, :nodes], history_ref[slot])) * (1.0 / fanout)).astype(
            BF16
        )
        for slot in range(slots)
    ]
    loads[2].wait()
    for slot in range(slots):
        term = matmul(means[slot], weight_ref[slot]).astype(BF16)
        term_ref[:, slot * part : (slot + 1) * part] = term.reshape(segments, part, width)
    stores = [pltpu.make_async_copy(term_ref, term_hbm, sems.at[3])]
    stores[0].start()
    for half in range(2):

        @pl.when(half_ref[0] == half)
        def _():
            for slot in range(slots):
                mean = means[slot]
                mine_ref[slot] = mean[:, half * width // 2 : (half + 1) * width // 2]
                others_ref[slot] = mean[:, (1 - half) * width // 2 : (2 - half) * width // 2]

    stores.append(pltpu.make_async_copy(mine_ref, mine_hbm, sems.at[4]))
    stores.append(pltpu.make_async_copy(others_ref, others_hbm, sems.at[5]))
    for store in stores[1:]:
        store.start()
    for store in stores:
        store.wait()


def normalize(pre_norm):
    inverse = lax.rsqrt(jnp.mean(pre_norm * pre_norm, axis=-1, keepdims=True) + epsilon)
    return inverse, pre_norm * inverse


def start_weights(segment_ref, pieces, weights, sems, order):
    for segment in range(len(order) // SLOTS):

        @pl.when(segment_ref[0] == segment)
        def _():
            for layer in order:
                section = layer // SLOTS
                ahead = (section // 2 - segment // 2) % 4
                piece = pieces[ahead * 2 + (section + segment) % 2]
                pltpu.make_async_copy(
                    piece.at[layer % SLOTS], weights.at[layer], sems.at[layer]
                ).start()


def wait_weights(pieces, weights, sems, layer):
    pltpu.make_async_copy(pieces[0].at[0], weights.at[layer], sems.at[layer]).wait()


def two_slots(terms_ref, section):
    rows = terms_ref.shape[1]
    return jnp.max(terms_ref[section, rows - 16 :, :128].astype(F32)) > 1.5


def layers_kernel(segment_ref, features_ref, cotangent_ref, terms_hbm, *refs):
    pieces, refs = refs[:8], refs[8:]
    out_hbm, out_ref, terms_ref, state, weights, pre, sems, term_sems, out_sems = refs
    segments, halves, _, _, slots, part, columns = out_ref.shape
    layers = segments * slots

    def load_terms(section):
        return pltpu.make_async_copy(
            terms_hbm.at[section], terms_ref.at[section], term_sems.at[section]
        )

    def store_rows(section):
        return pltpu.make_async_copy(
            out_ref.at[section], out_hbm.at[section], out_sems.at[section]
        )

    load_terms(0).start()
    start_weights(segment_ref, pieces, weights, sems, range(layers))
    for section in range(1, segments):
        load_terms(section).start()
    state[...] = features_ref[...]

    def keep_input(section, slot):
        x = state[...]
        for i in range(halves):
            for j in range(halves):
                out_ref[section, i, j, 0, slot] = x[:, i * columns : (i + 1) * columns]

    def forward(section, slot):
        layer = section * slots + slot
        x = state[...]
        pre_norm = matmul(x, weights[layer]) + terms_ref[
            section, slot * part : (slot + 1) * part
        ].astype(F32)
        pre[layer] = pre_norm
        _, normed = normalize(pre_norm)
        state[...] = (x.astype(F32) + normed * jax.nn.sigmoid(normed)).astype(BF16)

    @pl.loop(0, segments)
    def _(section):
        load_terms(section).wait()
        both = two_slots(terms_ref, section)
        wait_weights(pieces, weights, sems, section * slots)
        keep_input(section, 0)
        forward(section, 0)
        wait_weights(pieces, weights, sems, section * slots + 1)
        keep_input(section, 1)

        @pl.when(both)
        def _():
            forward(section, 1)

    state[...] = cotangent_ref[...]

    def backward(section, slot):
        layer = section * slots + slot
        inverse, normed = normalize(pre[layer])
        grad_out = state[...].astype(F32)
        sigmoid = jax.nn.sigmoid(normed)
        grad_normed = grad_out * sigmoid * (1.0 + normed * (1.0 - sigmoid))
        grad_pre = inverse * (
            grad_normed - normed * jnp.mean(grad_normed * normed, axis=-1, keepdims=True)
        )
        low = grad_pre.astype(BF16)
        for i in range(halves):
            for j in range(halves):
                out_ref[section, i, j, 1, slot] = low[:, j * columns : (j + 1) * columns]
        back = lax.dot_general(
            low, weights[layer], (((1,), (1,)), ((), ())), preferred_element_type=F32
        )
        state[...] = (grad_out + back).astype(BF16)

    @pl.loop(0, segments)
    def _(step):
        section = segments - 1 - step
        both = two_slots(terms_ref, section)

        @pl.when(both)
        def _():
            backward(section, 1)

        @pl.when(jnp.logical_not(both))
        def _():
            for i in range(halves):
                for j in range(halves):
                    out_ref[section, i, j, 1, 1] = jnp.zeros((part, columns), BF16)

        backward(section, 0)
        store_rows(section).start()

    for section in range(segments):
        store_rows(section).wait()


def product_kernel(
    place_ref, rows_ref, mean0, mean1, mean2, mean3, out_ref, own_ref, partner_ref
):
    segments, parts, _, slots, rows, columns = rows_ref.shape
    shards, _, _, out_rows, _ = out_ref.shape
    place = place_ref[0]
    own_ref[...] = rows_ref[:, place, 0]
    partner_ref[...] = rows_ref[:, place ^ 2, 0]
    for slot in range(slots):
        self_sum = neigh_sum = None
        for step, mean in enumerate((mean0, mean1, mean2, mean3)):
            part = place ^ step
            grad = rows_ref[:, part, 1, slot].reshape(segments * rows, columns).T
            layer_in = rows_ref[:, part, 0, slot].reshape(segments * rows, columns)
            self_term, neigh_term = matmul(grad, layer_in), matmul(grad, mean[slot])
            self_sum = self_term if self_sum is None else self_sum + self_term
            neigh_sum = neigh_term if neigh_sum is None else neigh_sum + neigh_term
        for kind, total in enumerate((self_sum, neigh_sum)):
            out_ref[:, kind, slot] = total.T.astype(BF16).reshape(shards, out_rows, columns)


def finish_kernel(half_ref, parts_ref, own_ref, missing_ref, self_ref, neigh_ref, out_ref):
    width = parts_ref.shape[5]
    for part in range(parts_ref.shape[0]):
        total = jnp.sum(parts_ref[part].astype(F32), axis=0)
        self_ref[:, :, part * width : (part + 1) * width] = total[0]
        neigh_ref[:, :, part * width : (part + 1) * width] = total[1]
    segments, slots, rows, columns = own_ref.shape
    for half in range(2):

        @pl.when(half_ref[0] == half)
        def _():
            for ref, at in ((own_ref, half), (missing_ref, 1 - half)):
                for slot in range(slots):
                    out_ref[slot, :, at * columns : (at + 1) * columns] = ref[:, slot].reshape(
                        segments * rows, columns
                    )


def round_y(block, step_of):
    size = lax.axis_size("segment")
    route = [(i, (i + 2 * step_of(i % 2)) % size) for i in range(size)]
    return lax.ppermute(block, "segment", route)


def core_swap(block):
    size = lax.axis_size("segment")
    return lax.ppermute(block, "segment", [(i, i ^ 1) for i in range(size)])


def x_swap(block, step):
    return lax.ppermute(block, ("xa", "xb"), [(i, i ^ step) for i in range(PAIR * PAIR)])


def exchange(block, axes):
    return lax.all_to_all(block, axes, split_axis=0, concat_axis=0, tiled=True)


def body(
    features,
    history,
    weight_self,
    weight_neigh,
    depth,
    send_index,
    pair_count,
    neighbours,
    cotangent,
):
    segments = lax.axis_size("segment")
    x_size = PAIR * PAIR
    z_size = lax.axis_size("z")
    shards = x_size * z_size
    my_segment = lax.axis_index("segment").reshape(1)
    my_half = lax.axis_index("xa").reshape(1)
    my_place = lax.axis_index(("xa", "xb")).reshape(1)
    my_shard = lax.axis_index(("xa", "xb", "z"))
    slots, nodes, width = history.shape
    rows_pair = send_index.shape[2]
    fanout = neighbours.shape[1]
    layers = segments * slots
    part = nodes // segments
    columns = width // 2
    received_rows = shards * rows_pair

    last_w = round_y(weight_self, lambda core: 1)
    next_w = round_y(weight_self, lambda core: -1)

    outgoing = pl.pallas_call(
        pick_kernel,
        out_shape=jax.ShapeDtypeStruct((shards, slots, rows_pair, width), BF16),
        compiler_params=params(12),
        name="pick_rows",
    )(send_index.reshape(received_rows, 1), history)
    received = exchange(outgoing, ("xa", "xb", "z"))

    own_rows = functools.partial(
        lax.dynamic_slice_in_dim, start_index=lax.axis_index("segment") * part, slice_size=part
    )
    my_features, my_cotangent, neighbours = lax.optimization_barrier(
        (own_rows(features), own_rows(cotangent), neighbours)
    )
    last_w, next_w, other_w, token = lax.optimization_barrier(
        (last_w, next_w, core_swap(weight_self), depth.reshape(1, 1))
    )
    token = pl.pallas_call(
        token_kernel,
        out_shape=jax.ShapeDtypeStruct((1, 1), jnp.int32),
        in_specs=[pl.BlockSpec(memory_space=pltpu.SMEM)],
        out_specs=pl.BlockSpec(memory_space=pltpu.SMEM),
        cost_estimate=lasting(40),
        name="after_first_wave",
    )(token)
    my_counts = lax.dynamic_index_in_dim(pair_count, my_shard, 1, keepdims=True)
    live = (lax.iota(jnp.int32, rows_pair)[None, :] < my_counts).astype(F32)
    live = jnp.concatenate(
        [jnp.ones((1, nodes), F32), live.reshape(1, received_rows)], axis=1
    )
    smem = pl.BlockSpec(memory_space=pltpu.SMEM)
    vmem = pl.BlockSpec(memory_space=pltpu.VMEM)
    hbm = pl.BlockSpec(memory_space=pltpu.MemorySpace.HBM)
    counts_shape = (nodes, nodes + received_rows)
    counts = pl.pallas_call(
        count_kernel,
        out_specs=hbm,
        out_shape=jax.ShapeDtypeStruct(counts_shape, BF16),
        scratch_shapes=[pltpu.VMEM(counts_shape, BF16), pltpu.SemaphoreType.DMA],
        compiler_params=params(12),
        cost_estimate=lasting(2),
        name="count_rows",
    )(neighbours, live)

    _, last_w, next_w = lax.optimization_barrier((token, last_w, next_w))
    forwarded = jnp.where(lax.rem(my_segment[0], 2) == 0, last_w, next_w)
    far_w = round_y(forwarded, lambda core: 1 - 2 * core)
    next_other, last_other = core_swap(next_w), core_swap(last_w)

    term_rows = slots * part + 16
    half_shape = jax.ShapeDtypeStruct((slots, nodes, columns), BF16)
    mean, others_mean, terms = pl.pallas_call(
        functools.partial(mean_kernel, fanout=fanout),
        in_specs=[smem, smem, vmem, hbm, hbm, hbm],
        out_specs=(hbm, hbm, hbm),
        scratch_shapes=[
            pltpu.VMEM(counts_shape, BF16),
            pltpu.VMEM(history.shape, BF16),
            pltpu.VMEM(weight_neigh.shape, BF16),
            pltpu.VMEM(half_shape.shape, BF16),
            pltpu.VMEM(half_shape.shape, BF16),
            pltpu.VMEM((segments, term_rows, width), BF16),
            pltpu.SemaphoreType.DMA((6,)),
        ],
        out_shape=(
            half_shape,
            half_shape,
            jax.ShapeDtypeStruct((segments, term_rows, width), BF16),
        ),
        compiler_params=params(59.3),
        cost_estimate=lasting(2),
        name="neighbour_mean",
    )(depth, my_half, received, counts, history, weight_neigh)
    all_terms = exchange(terms, "segment")
    _, far_w, next_other, last_other = lax.optimization_barrier(
        (mean, far_w, next_other, last_other)
    )
    pieces = (
        weight_self, other_w, next_w, next_other, far_w, core_swap(far_w), last_w, last_other
    )

    anywhere = pl.BlockSpec(memory_space=pl.ANY)
    rows = pl.pallas_call(
        layers_kernel,
        in_specs=[smem, vmem, vmem, anywhere] + [anywhere] * len(pieces),
        out_specs=anywhere,
        out_shape=jax.ShapeDtypeStruct((segments, 2, 2, 2, slots, part, columns), BF16),
        scratch_shapes=[
            pltpu.VMEM((segments, 2, 2, 2, slots, part, columns), BF16),
            pltpu.VMEM((segments, term_rows, width), BF16),
            pltpu.VMEM((part, width), BF16),
            pltpu.VMEM((layers, width, width), BF16),
            pltpu.VMEM((layers, part, width), F32),
            pltpu.SemaphoreType.DMA((layers,)),
            pltpu.SemaphoreType.DMA((segments,)),
            pltpu.SemaphoreType.DMA((segments,)),
        ],
        compiler_params=params(60),
        cost_estimate=lasting(13),
        name="all_layers",
    )(my_segment, my_features, my_cotangent, all_terms, *pieces)
    rows, *other_means = lax.optimization_barrier(
        (rows, x_swap(mean, 1), x_swap(others_mean, 2), x_swap(others_mean, 3))
    )
    means = (mean, *other_means)
    rows = rows.reshape(segments * x_size, 2, slots, part, columns)
    rows = exchange(rows, ("segment", "xa", "xb"))

    out_rows = width // shards
    sources = PAIR * z_size
    kept_shape = jax.ShapeDtypeStruct((segments, slots, part, columns), BF16)
    products, kept, for_partner = pl.pallas_call(
        product_kernel,
        in_specs=[smem] + [vmem] * 5,
        out_shape=(
            jax.ShapeDtypeStruct((sources, 2, slots, out_rows, columns), BF16),
            kept_shape,
            kept_shape,
        ),
        compiler_params=params(16),
        cost_estimate=lasting(3),
        name="weight_products",
    )(my_place, rows.reshape(segments, x_size, 2, slots, part, columns), *means)
    summands = exchange(products, ("xb", "z"))
    grad_shape = jax.ShapeDtypeStruct((slots, out_rows, width), F32)
    grad_self, grad_neigh, new_history = pl.pallas_call(
        finish_kernel,
        in_specs=[smem, vmem, vmem, vmem],
        out_shape=(grad_shape, grad_shape, jax.ShapeDtypeStruct((slots, nodes, width), BF16)),
        compiler_params=params(12),
        name="finish",
    )(
        my_half,
        summands.reshape(PAIR, z_size, 2, slots, out_rows, columns),
        kept,
        x_swap(for_partner, 2),
    )
    return (new_history, grad_self, grad_neigh)


def solution(mesh):
    segments, shards = mesh.devices.shape
    split = Mesh(
        mesh.devices.reshape(segments, PAIR, PAIR, shards // (PAIR * PAIR)),
        ("segment", "xa", "xb", "z"),
    )
    shard = ("xa", "xb", "z")
    return jax.shard_map(
        body,
        mesh=split,
        in_specs=(
            P(shard, None),
            P("segment", shard, None),
            P("segment", None, None),
            P("segment", None, None),
            P("segment"),
            P(shard, None, None),
            P(),
            P(shard, None),
            P(shard, None),
        ),
        out_specs=(
            P("segment", shard, None),
            P("segment", shard, None),
            P("segment", shard, None),
        ),
        check_vma=False,
    )
```

```python
import functools

import jax
import jax.numpy as jnp
from jax import lax
from jax.experimental import pallas as pl
from jax.experimental.pallas import tpu as pltpu
from jax.sharding import Mesh
from jax.sharding import PartitionSpec as P

epsilon = 1e-06
SLOTS = 2
PAIR = 2
BF16 = jnp.bfloat16
F32 = jnp.float32
MIB = 1024 * 1024
INACTIVE = 1e30
AHEAD = 3


def matmul(a, b):
    return jnp.dot(a, b, preferred_element_type=F32)


def params(mib):
    return pltpu.CompilerParams(vmem_limit_bytes=int(mib * MIB))


def lasting(microseconds):
    return pl.CostEstimate(
        flops=int(microseconds * 1.15e9), bytes_accessed=4 * MIB, transcendentals=0
    )


def pick_kernel(index_ref, history_ref, out_ref):
    slots, nodes, width = history_ref.shape
    shards, _, rows, _ = out_ref.shape
    columns = lax.broadcasted_iota(jnp.int32, (shards * rows, nodes), 1)
    chosen = (index_ref[...] == columns).astype(F32).astype(BF16)
    for slot in range(slots):
        picked = matmul(chosen, history_ref[slot]).astype(BF16)
        out_ref[:, slot] = picked.reshape(shards, rows, width)


def token_kernel(in_ref, out_ref):
    out_ref[0, 0] = in_ref[0, 0]


def count_kernel(neighbours_ref, live_ref, out_ref, counts_ref, sem):
    nodes, table = counts_ref.shape
    columns = lax.broadcasted_iota(jnp.int32, (nodes, table), 1)
    total = jnp.zeros((nodes, table), F32)
    for k in range(neighbours_ref.shape[1]):
        total += jnp.where(neighbours_ref[:, k : k + 1] == columns, 1.0, 0.0)
    counts_ref[...] = (total * live_ref[...]).astype(BF16)
    copy = pltpu.make_async_copy(counts_ref, out_ref, sem)
    copy.start()
    copy.wait()


def mean_kernel(
    depth_ref, half_ref, received_hbm, counts_hbm, history_hbm, weight_hbm,
    mine_hbm, others_hbm, term_hbm,
    received_ref, counts_ref, history_ref, weight_ref, mine_ref, others_ref, term_ref, sems, *, fanout,
):
    slots, nodes, width = history_ref.shape
    segments = term_ref.shape[0]
    part = nodes // segments
    loads = [
        pltpu.make_async_copy(hbm, ref, sems.at[i])
        for i, (hbm, ref) in enumerate(
            (
                (counts_hbm, counts_ref),
                (received_hbm, received_ref),
                (history_hbm, history_ref),
                (weight_hbm, weight_ref),
            )
        )
    ]
    for load in loads:
        load.start()
    loads[0].wait()
    loads[1].wait()
    far = [
        matmul(counts_ref[:, nodes:], received_ref[:, slot].reshape(-1, width))
        for slot in range(slots)
    ]
    loads[2].wait()
    means = [
        ((far[slot] + matmul(counts_ref[:, :nodes], history_ref[slot])) * (1.0 / fanout)).astype(
            BF16
        )
        for slot in range(slots)
    ]
    loads[3].wait()
    for slot in range(slots):
        term = matmul(means[slot], weight_ref[slot]).astype(BF16)
        if slot:
            term = jnp.where(slot < depth_ref[0], term, jnp.full_like(term, INACTIVE))
        term_ref[:, slot * part : (slot + 1) * part] = term.reshape(segments, part, width)
    stores = [pltpu.make_async_copy(term_ref, term_hbm, sems.at[4])]
    stores[0].start()
    for half in range(2):

        @pl.when(half_ref[0] == half)
        def _():
            for slot in range(slots):
                mean = means[slot]
                mine_ref[slot] = mean[:, half * width // 2 : (half + 1) * width // 2]
                others_ref[slot] = mean[:, (1 - half) * width // 2 : (2 - half) * width // 2]

    stores.append(pltpu.make_async_copy(mine_ref, mine_hbm, sems.at[5]))
    stores.append(pltpu.make_async_copy(others_ref, others_hbm, sems.at[6]))
    for store in stores[1:]:
        store.start()
    for store in stores:
        store.wait()


def normalize(pre_norm):
    inverse = lax.rsqrt(jnp.mean(pre_norm * pre_norm, axis=-1, keepdims=True) + epsilon)
    return inverse, pre_norm * inverse


def start_weights(segment_ref, pieces, weights, sems, section):
    mine = segment_ref[0]
    ahead = lax.rem(section // 2 - mine // 2 + 4, 4)
    index = ahead * 2 + lax.rem(section + mine, 2)
    for at, piece in enumerate(pieces):

        @pl.when(index == at)
        def _():
            weight_copy(piece, weights, sems, section).start()


def weight_copy(piece, weights, sems, section):
    slots = weights.at[pl.ds(section * SLOTS, SLOTS)]
    return pltpu.make_async_copy(piece, slots, sems.at[section])


def two_slots(terms_ref, section):
    part = terms_ref.shape[1] // SLOTS
    return jnp.max(terms_ref[section, part : part + 16, :128].astype(F32)) < INACTIVE / 2


def layers_kernel(segment_ref, features_hbm, cotangent_hbm, terms_hbm, *refs):
    pieces, refs = refs[:8], refs[8:]
    out_hbm, out_ref, terms_ref, state, cotangent, weights, pre, sems, term_sems, out_sems = refs
    segments, halves, _, _, slots, part, columns = out_ref.shape
    layers = segments * slots

    def load_terms(section):
        return pltpu.make_async_copy(
            terms_hbm.at[section], terms_ref.at[section], term_sems.at[section]
        )

    def store_rows(section):
        return pltpu.make_async_copy(
            out_ref.at[section], out_hbm.at[section], out_sems.at[section]
        )

    my_rows = pl.ds(pl.multiple_of(segment_ref[0] * part, part), part)
    load_features = pltpu.make_async_copy(features_hbm.at[my_rows], state, out_sems.at[0])
    load_cotangent = pltpu.make_async_copy(cotangent_hbm.at[my_rows], cotangent, out_sems.at[1])
    load_features.start()
    for section in range(AHEAD):
        start_weights(segment_ref, pieces, weights, sems, section)
    for section in range(segments):
        load_terms(section).start()
    load_cotangent.start()
    load_features.wait()

    def keep_input(section, slot):
        x = state[...]
        for i in range(halves):
            for j in range(halves):
                out_ref[section, i, j, 0, slot] = x[:, i * columns : (i + 1) * columns]

    def forward(section, slot):
        layer = section * slots + slot
        x = state[...]
        pre_norm = matmul(x, weights[layer]) + terms_ref[
            section, slot * part : (slot + 1) * part
        ].astype(F32)
        pre[layer] = pre_norm
        _, normed = normalize(pre_norm)
        state[...] = (x.astype(F32) + normed * (0.5 + 0.5 * jnp.tanh(0.5 * normed))).astype(BF16)

    @pl.loop(0, segments, unroll=8)
    def _(section):
        load_terms(section).wait()
        both = two_slots(terms_ref, section)
        weight_copy(pieces[0], weights, sems, section).wait()

        @pl.when(section + AHEAD < segments)
        def _():
            start_weights(segment_ref, pieces, weights, sems, section + AHEAD)

        keep_input(section, 0)
        forward(section, 0)
        keep_input(section, 1)

        @pl.when(both)
        def _():
            forward(section, 1)

    load_cotangent.wait()
    state[...] = cotangent[...]

    def backward(section, slot):
        layer = section * slots + slot
        inverse, normed = normalize(pre[layer])
        grad_out = state[...].astype(F32)
        sigmoid = (0.5 + 0.5 * jnp.tanh(0.5 * normed))
        grad_normed = grad_out * sigmoid * (1.0 + normed * (1.0 - sigmoid))
        grad_pre = inverse * (
            grad_normed - normed * jnp.mean(grad_normed * normed, axis=-1, keepdims=True)
        )
        low = grad_pre.astype(BF16)
        for i in range(halves):
            for j in range(halves):
                out_ref[section, i, j, 1, slot] = low[:, j * columns : (j + 1) * columns]
        back = lax.dot_general(
            low, weights[layer], (((1,), (1,)), ((), ())), preferred_element_type=F32
        )
        state[...] = (grad_out + back).astype(BF16)

    @pl.loop(0, segments, unroll=8)
    def _(step):
        section = segments - 1 - step
        both = two_slots(terms_ref, section)

        @pl.when(both)
        def _():
            backward(section, 1)

        @pl.when(jnp.logical_not(both))
        def _():
            for i in range(halves):
                for j in range(halves):
                    out_ref[section, i, j, 1, 1] = jnp.zeros((part, columns), BF16)

        backward(section, 0)
        store_rows(section).start()

    for section in range(segments):
        store_rows(section).wait()


def product_kernel(
    place_ref, rows_ref, mean0, mean1, mean2, mean3, out_ref, own_ref, partner_ref
):
    segments, parts, _, slots, rows, columns = rows_ref.shape
    shards, _, _, out_rows, _ = out_ref.shape
    place = place_ref[0]
    own_ref[...] = rows_ref[:, place, 0]
    partner_ref[...] = rows_ref[:, place ^ 2, 0]
    for slot in range(slots):
        self_sum = neigh_sum = None
        for step, mean in enumerate((mean0, mean1, mean2, mean3)):
            part = place ^ step
            grad = rows_ref[:, part, 1, slot].reshape(segments * rows, columns).T
            layer_in = rows_ref[:, part, 0, slot].reshape(segments * rows, columns)
            self_term, neigh_term = matmul(grad, layer_in), matmul(grad, mean[slot])
            self_sum = self_term if self_sum is None else self_sum + self_term
            neigh_sum = neigh_term if neigh_sum is None else neigh_sum + neigh_term
        for kind, total in enumerate((self_sum, neigh_sum)):
            out_ref[:, kind, slot] = total.T.astype(BF16).reshape(shards, out_rows, columns)


def finish_kernel(half_ref, parts_ref, own_ref, missing_ref, self_ref, neigh_ref, out_ref):
    width = parts_ref.shape[5]
    for part in range(parts_ref.shape[0]):
        total = jnp.sum(parts_ref[part].astype(F32), axis=0)
        self_ref[:, :, part * width : (part + 1) * width] = total[0]
        neigh_ref[:, :, part * width : (part + 1) * width] = total[1]
    segments, slots, rows, columns = own_ref.shape
    for half in range(2):

        @pl.when(half_ref[0] == half)
        def _():
            for ref, at in ((own_ref, half), (missing_ref, 1 - half)):
                for slot in range(slots):
                    out_ref[slot, :, at * columns : (at + 1) * columns] = ref[:, slot].reshape(
                        segments * rows, columns
                    )


def round_y(block, step_of):
    size = lax.axis_size("segment")
    route = [(i, (i + 2 * step_of(i % 2)) % size) for i in range(size)]
    return lax.ppermute(block, "segment", route)


def core_swap(block):
    size = lax.axis_size("segment")
    return lax.ppermute(block, "segment", [(i, i ^ 1) for i in range(size)])


def x_swap(block, step):
    return lax.ppermute(block, ("xa", "xb"), [(i, i ^ step) for i in range(PAIR * PAIR)])


def exchange(block, axes):
    return lax.all_to_all(block, axes, split_axis=0, concat_axis=0, tiled=True)


def body(
    features,
    history,
    weight_self,
    weight_neigh,
    depth,
    send_index,
    pair_count,
    neighbours,
    cotangent,
):
    segments = lax.axis_size("segment")
    x_size = PAIR * PAIR
    z_size = lax.axis_size("z")
    shards = x_size * z_size
    my_segment = lax.axis_index("segment").reshape(1)
    my_half = lax.axis_index("xa").reshape(1)
    my_place = lax.axis_index(("xa", "xb")).reshape(1)
    my_shard = lax.axis_index(("xa", "xb", "z"))
    slots, nodes, width = history.shape
    rows_pair = send_index.shape[2]
    fanout = neighbours.shape[1]
    layers = segments * slots
    part = nodes // segments
    columns = width // 2
    received_rows = shards * rows_pair

    last_w = round_y(weight_self, lambda core: 1)
    next_w = round_y(weight_self, lambda core: -1)

    outgoing = pl.pallas_call(
        pick_kernel,
        out_shape=jax.ShapeDtypeStruct((shards, slots, rows_pair, width), BF16),
        compiler_params=params(12),
        name="pick_rows",
    )(send_index.reshape(received_rows, 1), history)
    received = exchange(outgoing, ("xa", "xb", "z"))

    last_w, next_w, other_w, token = lax.optimization_barrier(
        (last_w, next_w, core_swap(weight_self), depth.reshape(1, 1))
    )
    token = pl.pallas_call(
        token_kernel,
        out_shape=jax.ShapeDtypeStruct((1, 1), jnp.int32),
        in_specs=[pl.BlockSpec(memory_space=pltpu.SMEM)],
        out_specs=pl.BlockSpec(memory_space=pltpu.SMEM),
        cost_estimate=lasting(40),
        name="after_first_wave",
    )(token)
    my_counts = lax.dynamic_index_in_dim(pair_count, my_shard, 1, keepdims=True)
    live = (lax.iota(jnp.int32, rows_pair)[None, :] < my_counts).astype(F32)
    live = jnp.concatenate(
        [jnp.ones((1, nodes), F32), live.reshape(1, received_rows)], axis=1
    )
    smem = pl.BlockSpec(memory_space=pltpu.SMEM)
    vmem = pl.BlockSpec(memory_space=pltpu.VMEM)
    hbm = pl.BlockSpec(memory_space=pltpu.MemorySpace.HBM)
    counts_shape = (nodes, nodes + received_rows)
    counts = pl.pallas_call(
        count_kernel,
        out_specs=hbm,
        out_shape=jax.ShapeDtypeStruct(counts_shape, BF16),
        scratch_shapes=[pltpu.VMEM(counts_shape, BF16), pltpu.SemaphoreType.DMA],
        compiler_params=params(12),
        cost_estimate=lasting(2),
        name="count_rows",
    )(neighbours, live)

    _, last_w, next_w = lax.optimization_barrier((token, last_w, next_w))
    forwarded = jnp.where(lax.rem(my_segment[0], 2) == 0, last_w, next_w)
    far_w = round_y(forwarded, lambda core: 1 - 2 * core)
    next_other, last_other = core_swap(next_w), core_swap(last_w)

    term_rows = slots * part
    half_shape = jax.ShapeDtypeStruct((slots, nodes, columns), BF16)
    mean, others_mean, terms = pl.pallas_call(
        functools.partial(mean_kernel, fanout=fanout),
        in_specs=[smem, smem, hbm, hbm, hbm, hbm],
        out_specs=(hbm, hbm, hbm),
        scratch_shapes=[
            pltpu.VMEM(received.shape, BF16),
            pltpu.VMEM(counts_shape, BF16),
            pltpu.VMEM(history.shape, BF16),
            pltpu.VMEM(weight_neigh.shape, BF16),
            pltpu.VMEM(half_shape.shape, BF16),
            pltpu.VMEM(half_shape.shape, BF16),
            pltpu.VMEM((segments, term_rows, width), BF16),
            pltpu.SemaphoreType.DMA((7,)),
        ],
        out_shape=(
            half_shape,
            half_shape,
            jax.ShapeDtypeStruct((segments, term_rows, width), BF16),
        ),
        compiler_params=params(59.3),
        cost_estimate=lasting(2),
        name="neighbour_mean",
    )(depth, my_half, received, counts, history, weight_neigh)
    all_terms = exchange(terms, "segment")
    _, far_w, next_other, last_other = lax.optimization_barrier(
        (mean, far_w, next_other, last_other)
    )
    pieces = (
        weight_self, other_w, next_w, next_other, far_w, core_swap(far_w), last_w, last_other
    )

    anywhere = pl.BlockSpec(memory_space=pl.ANY)
    rows = pl.pallas_call(
        layers_kernel,
        in_specs=[smem] + [anywhere] * (3 + len(pieces)),
        out_specs=anywhere,
        out_shape=jax.ShapeDtypeStruct((segments, 2, 2, 2, slots, part, columns), BF16),
        scratch_shapes=[
            pltpu.VMEM((segments, 2, 2, 2, slots, part, columns), BF16),
            pltpu.VMEM((segments, term_rows, width), BF16),
            pltpu.VMEM((part, width), BF16),
            pltpu.VMEM((part, width), BF16),
            pltpu.VMEM((layers, width, width), BF16),
            pltpu.VMEM((layers, part, width), F32),
            pltpu.SemaphoreType.DMA((segments,)),
            pltpu.SemaphoreType.DMA((segments,)),
            pltpu.SemaphoreType.DMA((segments,)),
        ],
        compiler_params=params(57.5),
        cost_estimate=lasting(13),
        name="all_layers",
    )(my_segment, features, cotangent, all_terms, *pieces)
    rows, *other_means = lax.optimization_barrier(
        (rows, x_swap(mean, 1), x_swap(others_mean, 2), x_swap(others_mean, 3))
    )
    means = (mean, *other_means)
    rows = rows.reshape(segments * x_size, 2, slots, part, columns)
    rows = exchange(rows, ("segment", "xa", "xb"))

    out_rows = width // shards
    sources = PAIR * z_size
    kept_shape = jax.ShapeDtypeStruct((segments, slots, part, columns), BF16)
    products, kept, for_partner = pl.pallas_call(
        product_kernel,
        in_specs=[smem] + [vmem] * 5,
        out_shape=(
            jax.ShapeDtypeStruct((sources, 2, slots, out_rows, columns), BF16),
            kept_shape,
            kept_shape,
        ),
        compiler_params=params(16),
        cost_estimate=lasting(3),
        name="weight_products",
    )(my_place, rows.reshape(segments, x_size, 2, slots, part, columns), *means)
    summands = exchange(products, ("xb", "z"))
    grad_shape = jax.ShapeDtypeStruct((slots, out_rows, width), F32)
    grad_self, grad_neigh, new_history = pl.pallas_call(
        finish_kernel,
        in_specs=[smem, vmem, vmem, vmem],
        out_shape=(grad_shape, grad_shape, jax.ShapeDtypeStruct((slots, nodes, width), BF16)),
        compiler_params=params(12),
        name="finish",
    )(
        my_half,
        summands.reshape(PAIR, z_size, 2, slots, out_rows, columns),
        kept,
        x_swap(for_partner, 2),
    )
    return (new_history, grad_self, grad_neigh)


def solution(mesh):
    segments, shards = mesh.devices.shape
    split = Mesh(
        mesh.devices.reshape(segments, PAIR, PAIR, shards // (PAIR * PAIR)),
        ("segment", "xa", "xb", "z"),
    )
    shard = ("xa", "xb", "z")
    return jax.shard_map(
        body,
        mesh=split,
        in_specs=(
            P(shard, None),
            P("segment", shard, None),
            P("segment", None, None),
            P("segment", None, None),
            P("segment"),
            P(shard, None, None),
            P(),
            P(shard, None),
            P(shard, None),
        ),
        out_specs=(
            P("segment", shard, None),
            P("segment", shard, None),
            P("segment", shard, None),
        ),
        check_vma=False,
    )
```

```python
import functools

import jax
import jax.numpy as jnp
from jax import lax
from jax.experimental import pallas as pl
from jax.experimental.pallas import tpu as pltpu
from jax.sharding import Mesh
from jax.sharding import PartitionSpec as P

epsilon = 1e-06
SLOTS = 2
PAIR = 2
BF16 = jnp.bfloat16
F32 = jnp.float32
MIB = 1024 * 1024
INACTIVE = 1e30
AHEAD = 3


def matmul(a, b):
    return jnp.dot(a, b, preferred_element_type=F32)


def params(mib):
    return pltpu.CompilerParams(vmem_limit_bytes=int(mib * MIB))


def lasting(microseconds):
    return pl.CostEstimate(
        flops=int(microseconds * 1.15e9), bytes_accessed=4 * MIB, transcendentals=0
    )


def pick_kernel(index_ref, history_ref, out_ref):
    slots, nodes, width = history_ref.shape
    shards, _, rows, _ = out_ref.shape
    columns = lax.broadcasted_iota(jnp.int32, (shards * rows, nodes), 1)
    chosen = (index_ref[...] == columns).astype(F32).astype(BF16)
    for slot in range(slots):
        picked = matmul(chosen, history_ref[slot]).astype(BF16)
        out_ref[:, slot] = picked.reshape(shards, rows, width)


def token_kernel(in_ref, out_ref):
    out_ref[0, 0] = in_ref[0, 0]


def count_kernel(neighbours_ref, live_ref, out_ref, counts_ref, sem):
    nodes, table = counts_ref.shape
    columns = lax.broadcasted_iota(jnp.int32, (nodes, table), 1)
    total = jnp.zeros((nodes, table), F32)
    for k in range(neighbours_ref.shape[1]):
        total += jnp.where(neighbours_ref[:, k : k + 1] == columns, 1.0, 0.0)
    counts_ref[...] = (total * live_ref[...]).astype(BF16)
    copy = pltpu.make_async_copy(counts_ref, out_ref, sem)
    copy.start()
    copy.wait()


def mean_kernel(
    depth_ref, half_ref, received_hbm, counts_hbm, history_hbm, weight_hbm,
    mine_hbm, others_hbm, term_hbm,
    received_ref, counts_ref, history_ref, weight_ref, mine_ref, others_ref, term_ref, sems, *, fanout,
):
    slots, nodes, width = history_ref.shape
    segments = term_ref.shape[0]
    part = nodes // segments
    loads = [
        pltpu.make_async_copy(hbm, ref, sems.at[i])
        for i, (hbm, ref) in enumerate(
            (
                (counts_hbm, counts_ref),
                (received_hbm, received_ref),
                (history_hbm, history_ref),
                (weight_hbm, weight_ref),
            )
        )
    ]
    for load in loads:
        load.start()
    loads[0].wait()
    loads[1].wait()
    far = [
        matmul(counts_ref[:, nodes:], received_ref[:, slot].reshape(-1, width))
        for slot in range(slots)
    ]
    loads[2].wait()
    means = [
        ((far[slot] + matmul(counts_ref[:, :nodes], history_ref[slot])) * (1.0 / fanout)).astype(
            BF16
        )
        for slot in range(slots)
    ]
    loads[3].wait()
    for slot in range(slots):
        term = matmul(means[slot], weight_ref[slot]).astype(BF16)
        if slot:
            term = jnp.where(slot < depth_ref[0], term, jnp.full_like(term, INACTIVE))
        term_ref[:, slot * part : (slot + 1) * part] = term.reshape(segments, part, width)
    stores = [pltpu.make_async_copy(term_ref, term_hbm, sems.at[4])]
    stores[0].start()
    for half in range(2):

        @pl.when(half_ref[0] == half)
        def _():
            for slot in range(slots):
                mean = means[slot]
                mine_ref[slot] = mean[:, half * width // 2 : (half + 1) * width // 2]
                others_ref[slot] = mean[:, (1 - half) * width // 2 : (2 - half) * width // 2]

    stores.append(pltpu.make_async_copy(mine_ref, mine_hbm, sems.at[5]))
    stores.append(pltpu.make_async_copy(others_ref, others_hbm, sems.at[6]))
    for store in stores[1:]:
        store.start()
    for store in stores:
        store.wait()


def normalize(pre_norm):
    inverse = lax.rsqrt(jnp.mean(pre_norm * pre_norm, axis=-1, keepdims=True) + epsilon)
    return inverse, pre_norm * inverse


def start_weights(segment_ref, pieces, weights, sems, section):
    mine = segment_ref[0]
    ahead = lax.rem(section // 2 - mine // 2 + 4, 4)
    index = ahead * 2 + lax.rem(section + mine, 2)
    for at, piece in enumerate(pieces):

        @pl.when(index == at)
        def _():
            weight_copy(piece, weights, sems, section).start()


def weight_copy(piece, weights, sems, section):
    slots = weights.at[pl.ds(section * SLOTS, SLOTS)]
    return pltpu.make_async_copy(piece, slots, sems.at[section])


def two_slots(terms_ref, section):
    part = terms_ref.shape[1] // SLOTS
    return jnp.max(terms_ref[section, part : part + 16, :128].astype(F32)) < INACTIVE / 2


def layers_kernel(segment_ref, features_hbm, cotangent_hbm, terms_ref, *refs):
    pieces, refs = refs[:8], refs[8:]
    out_hbm, out_ref, state, cotangent, weights, kept_normed, slopes, sems, out_sems = refs
    _, _, slots, part, columns = out_ref.shape
    segments, halves = terms_ref.shape[0], 2
    layers = segments * slots

    def store_rows(section):
        rows = pl.ds(section * halves * halves, halves * halves)
        return pltpu.make_async_copy(out_ref.at[rows], out_hbm.at[rows], out_sems.at[section])

    my_rows = pl.ds(pl.multiple_of(segment_ref[0] * part, part), part)
    load_features = pltpu.make_async_copy(features_hbm.at[my_rows], state, out_sems.at[0])
    load_cotangent = pltpu.make_async_copy(cotangent_hbm.at[my_rows], cotangent, out_sems.at[1])
    load_features.start()
    for section in range(AHEAD):
        start_weights(segment_ref, pieces, weights, sems, section)
    load_cotangent.start()
    load_features.wait()

    def keep_input(section, slot):
        x = state[...]
        for i in range(halves):
            for j in range(halves):
                out_ref[(section * halves + i) * halves + j, 0, slot] = x[:, i * columns : (i + 1) * columns]

    def forward(section, slot):
        layer = section * slots + slot
        x = state[...]
        pre_norm = matmul(x, weights[layer]) + terms_ref[
            section, slot * part : (slot + 1) * part
        ].astype(F32)
        inverse, normed = normalize(pre_norm)
        sigmoid = 0.5 + 0.5 * jnp.tanh(0.5 * normed)
        state[...] = (x.astype(F32) + normed * sigmoid).astype(BF16)
        kept_normed[layer] = normed
        slopes[layer] = inverse * (sigmoid * (1.0 + normed * (1.0 - sigmoid)))

    @pl.loop(0, segments, unroll=8)
    def _(section):
        both = two_slots(terms_ref, section)
        weight_copy(pieces[0], weights, sems, section).wait()

        @pl.when(section + AHEAD < segments)
        def _():
            start_weights(segment_ref, pieces, weights, sems, section + AHEAD)

        keep_input(section, 0)
        forward(section, 0)
        keep_input(section, 1)

        @pl.when(both)
        def _():
            forward(section, 1)

    load_cotangent.wait()
    state[...] = cotangent[...]

    def backward(section, slot):
        layer = section * slots + slot
        normed = kept_normed[layer]
        grad_out = state[...].astype(F32)
        scaled = grad_out * slopes[layer]
        grad_pre = scaled - normed * jnp.mean(scaled * normed, axis=-1, keepdims=True)
        low = grad_pre.astype(BF16)
        for i in range(halves):
            for j in range(halves):
                out_ref[(section * halves + i) * halves + j, 1, slot] = low[:, j * columns : (j + 1) * columns]
        back = lax.dot_general(
            low, weights[layer], (((1,), (1,)), ((), ())), preferred_element_type=F32
        )
        state[...] = (grad_out + back).astype(BF16)

    @pl.loop(0, segments, unroll=8)
    def _(step):
        section = segments - 1 - step
        both = two_slots(terms_ref, section)

        @pl.when(both)
        def _():
            backward(section, 1)

        @pl.when(jnp.logical_not(both))
        def _():
            for i in range(halves):
                for j in range(halves):
                    out_ref[(section * halves + i) * halves + j, 1, 1] = jnp.zeros((part, columns), BF16)

        backward(section, 0)
        store_rows(section).start()

    for section in range(segments):
        store_rows(section).wait()


def product_kernel(
    place_ref, rows_ref, mean0, mean1, mean2, mean3, out_ref, own_ref, partner_ref
):
    segments, parts, _, slots, rows, columns = rows_ref.shape
    shards, _, _, out_rows, _ = out_ref.shape
    place = place_ref[0]
    own_ref[...] = rows_ref[:, place, 0]
    partner_ref[...] = rows_ref[:, place ^ 2, 0]
    for slot in range(slots):
        self_sum = neigh_sum = None
        for step, mean in enumerate((mean0, mean1, mean2, mean3)):
            part = place ^ step
            grad = rows_ref[:, part, 1, slot].reshape(segments * rows, columns).T
            layer_in = rows_ref[:, part, 0, slot].reshape(segments * rows, columns)
            self_term, neigh_term = matmul(grad, layer_in), matmul(grad, mean[slot])
            self_sum = self_term if self_sum is None else self_sum + self_term
            neigh_sum = neigh_term if neigh_sum is None else neigh_sum + neigh_term
        for kind, total in enumerate((self_sum, neigh_sum)):
            out_ref[:, kind, slot] = total.T.astype(BF16).reshape(shards, out_rows, columns)


def finish_kernel(half_ref, parts_ref, own_ref, missing_ref, self_ref, neigh_ref, out_ref):
    width = parts_ref.shape[5]
    for part in range(parts_ref.shape[0]):
        total = jnp.sum(parts_ref[part].astype(F32), axis=0)
        self_ref[:, :, part * width : (part + 1) * width] = total[0]
        neigh_ref[:, :, part * width : (part + 1) * width] = total[1]
    segments, slots, rows, columns = own_ref.shape
    for half in range(2):

        @pl.when(half_ref[0] == half)
        def _():
            for ref, at in ((own_ref, half), (missing_ref, 1 - half)):
                for slot in range(slots):
                    out_ref[slot, :, at * columns : (at + 1) * columns] = ref[:, slot].reshape(
                        segments * rows, columns
                    )


def round_y(block, step_of):
    size = lax.axis_size("segment")
    route = [(i, (i + 2 * step_of(i % 2)) % size) for i in range(size)]
    return lax.ppermute(block, "segment", route)


def core_swap(block):
    size = lax.axis_size("segment")
    return lax.ppermute(block, "segment", [(i, i ^ 1) for i in range(size)])


def x_swap(block, step):
    return lax.ppermute(block, ("xa", "xb"), [(i, i ^ step) for i in range(PAIR * PAIR)])


def exchange(block, axes):
    return lax.all_to_all(block, axes, split_axis=0, concat_axis=0, tiled=True)


def body(
    features,
    history,
    weight_self,
    weight_neigh,
    depth,
    send_index,
    pair_count,
    neighbours,
    cotangent,
):
    segments = lax.axis_size("segment")
    x_size = PAIR * PAIR
    z_size = lax.axis_size("z")
    shards = x_size * z_size
    my_segment = lax.axis_index("segment").reshape(1)
    my_half = lax.axis_index("xa").reshape(1)
    my_place = lax.axis_index(("xa", "xb")).reshape(1)
    my_shard = lax.axis_index(("xa", "xb", "z"))
    slots, nodes, width = history.shape
    rows_pair = send_index.shape[2]
    fanout = neighbours.shape[1]
    layers = segments * slots
    part = nodes // segments
    columns = width // 2
    received_rows = shards * rows_pair

    last_w = round_y(weight_self, lambda core: 1)
    next_w = round_y(weight_self, lambda core: -1)

    outgoing = pl.pallas_call(
        pick_kernel,
        out_shape=jax.ShapeDtypeStruct((shards, slots, rows_pair, width), BF16),
        compiler_params=params(12),
        name="pick_rows",
    )(send_index.reshape(received_rows, 1), history)
    received = exchange(outgoing, ("xa", "xb", "z"))

    last_w, next_w, other_w, token = lax.optimization_barrier(
        (last_w, next_w, core_swap(weight_self), depth.reshape(1, 1))
    )
    token = pl.pallas_call(
        token_kernel,
        out_shape=jax.ShapeDtypeStruct((1, 1), jnp.int32),
        in_specs=[pl.BlockSpec(memory_space=pltpu.SMEM)],
        out_specs=pl.BlockSpec(memory_space=pltpu.SMEM),
        cost_estimate=lasting(40),
        name="after_first_wave",
    )(token)
    my_counts = lax.dynamic_index_in_dim(pair_count, my_shard, 1, keepdims=True)
    live = (lax.iota(jnp.int32, rows_pair)[None, :] < my_counts).astype(F32)
    live = jnp.concatenate(
        [jnp.ones((1, nodes), F32), live.reshape(1, received_rows)], axis=1
    )
    smem = pl.BlockSpec(memory_space=pltpu.SMEM)
    vmem = pl.BlockSpec(memory_space=pltpu.VMEM)
    hbm = pl.BlockSpec(memory_space=pltpu.MemorySpace.HBM)
    counts_shape = (nodes, nodes + received_rows)
    counts = pl.pallas_call(
        count_kernel,
        out_specs=hbm,
        out_shape=jax.ShapeDtypeStruct(counts_shape, BF16),
        scratch_shapes=[pltpu.VMEM(counts_shape, BF16), pltpu.SemaphoreType.DMA],
        compiler_params=params(12),
        cost_estimate=lasting(2),
        name="count_rows",
    )(neighbours, live)

    _, last_w, next_w = lax.optimization_barrier((token, last_w, next_w))
    forwarded = jnp.where(lax.rem(my_segment[0], 2) == 0, last_w, next_w)
    far_w = round_y(forwarded, lambda core: 1 - 2 * core)
    next_other, last_other = core_swap(next_w), core_swap(last_w)

    term_rows = slots * part
    half_shape = jax.ShapeDtypeStruct((slots, nodes, columns), BF16)
    mean, others_mean, terms = pl.pallas_call(
        functools.partial(mean_kernel, fanout=fanout),
        in_specs=[smem, smem, hbm, hbm, hbm, hbm],
        out_specs=(hbm, hbm, hbm),
        scratch_shapes=[
            pltpu.VMEM(received.shape, BF16),
            pltpu.VMEM(counts_shape, BF16),
            pltpu.VMEM(history.shape, BF16),
            pltpu.VMEM(weight_neigh.shape, BF16),
            pltpu.VMEM(half_shape.shape, BF16),
            pltpu.VMEM(half_shape.shape, BF16),
            pltpu.VMEM((segments, term_rows, width), BF16),
            pltpu.SemaphoreType.DMA((7,)),
        ],
        out_shape=(
            half_shape,
            half_shape,
            jax.ShapeDtypeStruct((segments, term_rows, width), BF16),
        ),
        compiler_params=params(59.3),
        cost_estimate=lasting(2),
        name="neighbour_mean",
    )(depth, my_half, received, counts, history, weight_neigh)
    all_terms = exchange(terms, "segment")
    _, far_w, next_other, last_other = lax.optimization_barrier(
        (mean, far_w, next_other, last_other)
    )
    pieces = (
        weight_self, other_w, next_w, next_other, far_w, core_swap(far_w), last_w, last_other
    )

    anywhere = pl.BlockSpec(memory_space=pl.ANY)
    rows = pl.pallas_call(
        layers_kernel,
        in_specs=[smem, anywhere, anywhere, vmem] + [anywhere] * len(pieces),
        out_specs=anywhere,
        out_shape=jax.ShapeDtypeStruct((segments * x_size, 2, slots, part, columns), BF16),
        scratch_shapes=[
            pltpu.VMEM((segments * x_size, 2, slots, part, columns), BF16),
            pltpu.VMEM((part, width), BF16),
            pltpu.VMEM((part, width), BF16),
            pltpu.VMEM((layers, width, width), BF16),
            pltpu.VMEM((layers, part, width), F32),
            pltpu.VMEM((layers, part, width), F32),
            pltpu.SemaphoreType.DMA((segments,)),
            pltpu.SemaphoreType.DMA((segments,)),
        ],
        compiler_params=params(50),
        cost_estimate=lasting(13),
        name="all_layers",
    )(my_segment, features, cotangent, all_terms, *pieces)
    rows, *other_means = lax.optimization_barrier(
        (rows, x_swap(mean, 1), x_swap(others_mean, 2), x_swap(others_mean, 3))
    )
    means = (mean, *other_means)
    rows = exchange(rows, ("segment", "xa", "xb"))

    out_rows = width // shards
    sources = PAIR * z_size
    kept_shape = jax.ShapeDtypeStruct((segments, slots, part, columns), BF16)
    products, kept, for_partner = pl.pallas_call(
        product_kernel,
        in_specs=[smem] + [vmem] * 5,
        out_shape=(
            jax.ShapeDtypeStruct((sources, 2, slots, out_rows, columns), BF16),
            kept_shape,
            kept_shape,
        ),
        compiler_params=params(16),
        cost_estimate=lasting(3),
        name="weight_products",
    )(my_place, rows.reshape(segments, x_size, 2, slots, part, columns), *means)
    summands = exchange(products, ("xb", "z"))
    grad_shape = jax.ShapeDtypeStruct((slots, out_rows, width), F32)
    grad_self, grad_neigh, new_history = pl.pallas_call(
        finish_kernel,
        in_specs=[smem, vmem, vmem, vmem],
        out_shape=(grad_shape, grad_shape, jax.ShapeDtypeStruct((slots, nodes, width), BF16)),
        compiler_params=params(12),
        name="finish",
    )(
        my_half,
        summands.reshape(PAIR, z_size, 2, slots, out_rows, columns),
        kept,
        x_swap(for_partner, 2),
    )
    return (new_history, grad_self, grad_neigh)


def solution(mesh):
    segments, shards = mesh.devices.shape
    split = Mesh(
        mesh.devices.reshape(segments, PAIR, PAIR, shards // (PAIR * PAIR)),
        ("segment", "xa", "xb", "z"),
    )
    shard = ("xa", "xb", "z")
    return jax.shard_map(
        body,
        mesh=split,
        in_specs=(
            P(shard, None),
            P("segment", shard, None),
            P("segment", None, None),
            P("segment", None, None),
            P("segment"),
            P(shard, None, None),
            P(),
            P(shard, None),
            P(shard, None),
        ),
        out_specs=(
            P("segment", shard, None),
            P("segment", shard, None),
            P("segment", shard, None),
        ),
        check_vma=False,
    )
```

```python
import functools

import jax
import jax.numpy as jnp
from jax import lax
from jax.experimental import pallas as pl
from jax.experimental.pallas import tpu as pltpu
from jax.sharding import Mesh
from jax.sharding import PartitionSpec as P

epsilon = 1e-06
SLOTS = 2
PAIR = 2
BF16 = jnp.bfloat16
F32 = jnp.float32
MIB = 1024 * 1024
INACTIVE = 1e30
AHEAD = 3


def matmul(a, b):
    return jnp.dot(a, b, preferred_element_type=F32)


def params(mib):
    return pltpu.CompilerParams(vmem_limit_bytes=int(mib * MIB))


def lasting(microseconds):
    return pl.CostEstimate(
        flops=int(microseconds * 1.15e9), bytes_accessed=4 * MIB, transcendentals=0
    )


def pick_kernel(index_ref, history_ref, out_ref):
    slots, nodes, width = history_ref.shape
    shards, _, rows, _ = out_ref.shape
    columns = lax.broadcasted_iota(jnp.int32, (shards * rows, nodes), 1)
    chosen = (index_ref[...] == columns).astype(F32).astype(BF16)
    for slot in range(slots):
        picked = matmul(chosen, history_ref[slot]).astype(BF16)
        out_ref[:, slot] = picked.reshape(shards, rows, width)


def token_kernel(in_ref, out_ref):
    out_ref[0, 0] = in_ref[0, 0]


def count_kernel(neighbours_ref, live_ref, out_ref, counts_ref, sem):
    nodes, table = counts_ref.shape
    columns = lax.broadcasted_iota(jnp.int32, (nodes, table), 1)
    total = jnp.zeros((nodes, table), F32)
    for k in range(neighbours_ref.shape[1]):
        total += jnp.where(neighbours_ref[:, k : k + 1] == columns, 1.0, 0.0)
    counts_ref[...] = (total * live_ref[...]).astype(BF16)
    copy = pltpu.make_async_copy(counts_ref, out_ref, sem)
    copy.start()
    copy.wait()


def mean_kernel(
    depth_ref, half_ref, received_hbm, counts_hbm, history_hbm, weight_hbm,
    mine_hbm, others_hbm, term_hbm,
    received_ref, counts_ref, history_ref, weight_ref, mine_ref, others_ref, term_ref, sems, *, fanout,
):
    slots, nodes, width = history_ref.shape
    segments = term_ref.shape[0]
    part = nodes // segments
    loads = [
        pltpu.make_async_copy(hbm, ref, sems.at[i])
        for i, (hbm, ref) in enumerate(
            (
                (counts_hbm, counts_ref),
                (received_hbm, received_ref),
                (history_hbm, history_ref),
                (weight_hbm, weight_ref),
            )
        )
    ]
    for load in loads:
        load.start()
    loads[0].wait()
    loads[1].wait()
    far = [
        matmul(counts_ref[:, nodes:], received_ref[:, slot].reshape(-1, width))
        for slot in range(slots)
    ]
    loads[2].wait()
    means = [
        ((far[slot] + matmul(counts_ref[:, :nodes], history_ref[slot])) * (1.0 / fanout)).astype(
            BF16
        )
        for slot in range(slots)
    ]
    loads[3].wait()
    for slot in range(slots):
        term = matmul(means[slot], weight_ref[slot]).astype(BF16)
        if slot:
            term = jnp.where(slot < depth_ref[0], term, jnp.full_like(term, INACTIVE))
        term_ref[:, slot * part : (slot + 1) * part] = term.reshape(segments, part, width)
    stores = [pltpu.make_async_copy(term_ref, term_hbm, sems.at[4])]
    stores[0].start()
    for half in range(2):

        @pl.when(half_ref[0] == half)
        def _():
            for slot in range(slots):
                mean = means[slot]
                mine_ref[slot] = mean[:, half * width // 2 : (half + 1) * width // 2]
                others_ref[slot] = mean[:, (1 - half) * width // 2 : (2 - half) * width // 2]

    stores.append(pltpu.make_async_copy(mine_ref, mine_hbm, sems.at[5]))
    stores.append(pltpu.make_async_copy(others_ref, others_hbm, sems.at[6]))
    for store in stores[1:]:
        store.start()
    for store in stores:
        store.wait()


def normalize(pre_norm):
    inverse = lax.rsqrt(jnp.mean(pre_norm * pre_norm, axis=-1, keepdims=True) + epsilon)
    return inverse, pre_norm * inverse


def start_weights(segment_ref, pieces, weights, sems, section):
    mine = segment_ref[0]
    ahead = lax.rem(section // 2 - mine // 2 + 4, 4)
    index = ahead * 2 + lax.rem(section + mine, 2)
    for at, piece in enumerate(pieces):

        @pl.when(index == at)
        def _():
            weight_copy(piece, weights, sems, section).start()


def weight_copy(piece, weights, sems, section):
    slots = weights.at[pl.ds(section * SLOTS, SLOTS)]
    return pltpu.make_async_copy(piece, slots, sems.at[section])


def two_slots(terms_ref, section):
    part = terms_ref.shape[1] // SLOTS
    return jnp.max(terms_ref[section, part : part + 16, :128].astype(F32)) < INACTIVE / 2


def layers_kernel(segment_ref, features_hbm, cotangent_hbm, terms_ref, *refs):
    pieces, refs = refs[:8], refs[8:]
    out_hbm, out_ref, state, cotangent, weights, kept_normed, slopes, sems, out_sems = refs
    _, _, slots, part, columns = out_ref.shape
    segments, halves = terms_ref.shape[0], 2
    layers = segments * slots

    def store_rows(section):
        rows = pl.ds(section * halves * halves, halves * halves)
        return pltpu.make_async_copy(out_ref.at[rows], out_hbm.at[rows], out_sems.at[section])

    my_rows = pl.ds(pl.multiple_of(segment_ref[0] * part, part), part)
    load_features = pltpu.make_async_copy(features_hbm.at[my_rows], state, out_sems.at[0])
    load_cotangent = pltpu.make_async_copy(cotangent_hbm.at[my_rows], cotangent, out_sems.at[1])
    load_features.start()
    for section in range(AHEAD):
        start_weights(segment_ref, pieces, weights, sems, section)
    load_cotangent.start()
    load_features.wait()

    def keep_input(section, slot):
        x = state[...]
        for i in range(halves):
            for j in range(halves):
                out_ref[(section * halves + i) * halves + j, 0, slot] = x[:, i * columns : (i + 1) * columns]

    def forward(section, slot):
        layer = section * slots + slot
        x = state[...]
        pre_norm = matmul(x, weights[layer]) + terms_ref[
            section, slot * part : (slot + 1) * part
        ].astype(F32)
        inverse, normed = normalize(pre_norm)
        sigmoid = 0.5 + 0.5 * jnp.tanh(0.5 * normed)
        state[...] = (x.astype(F32) + normed * sigmoid).astype(BF16)
        kept_normed[layer] = normed
        slopes[layer] = inverse * (sigmoid * (1.0 + normed * (1.0 - sigmoid)))

    @pl.loop(0, segments, unroll=8)
    def _(section):
        both = two_slots(terms_ref, section)
        weight_copy(pieces[0], weights, sems, section).wait()

        @pl.when(section + AHEAD < segments)
        def _():
            start_weights(segment_ref, pieces, weights, sems, section + AHEAD)

        keep_input(section, 0)
        forward(section, 0)
        keep_input(section, 1)

        @pl.when(both)
        def _():
            forward(section, 1)

    load_cotangent.wait()
    state[...] = cotangent[...]

    def backward(section, slot):
        layer = section * slots + slot
        normed = kept_normed[layer]
        grad_out = state[...].astype(F32)
        scaled = grad_out * slopes[layer]
        grad_pre = scaled - normed * jnp.mean(scaled * normed, axis=-1, keepdims=True)
        low = grad_pre.astype(BF16)
        for i in range(halves):
            for j in range(halves):
                out_ref[(section * halves + i) * halves + j, 1, slot] = low[:, j * columns : (j + 1) * columns]
        back = lax.dot_general(
            low, weights[layer], (((1,), (1,)), ((), ())), preferred_element_type=F32
        )
        state[...] = (grad_out + back).astype(BF16)

    @pl.loop(0, segments, unroll=8)
    def _(step):
        section = segments - 1 - step
        both = two_slots(terms_ref, section)

        @pl.when(both)
        def _():
            backward(section, 1)

        @pl.when(jnp.logical_not(both))
        def _():
            for i in range(halves):
                for j in range(halves):
                    out_ref[(section * halves + i) * halves + j, 1, 1] = jnp.zeros((part, columns), BF16)

        backward(section, 0)
        store_rows(section).start()

    for section in range(segments):
        store_rows(section).wait()


def product_kernel(
    place_ref, rows_ref, mean0, mean1, mean2, mean3, out_ref, own_ref, partner_ref
):
    segments, parts, _, slots, rows, columns = rows_ref.shape
    shards, _, _, out_rows, _ = out_ref.shape
    place = place_ref[0]
    own_ref[...] = rows_ref[:, place, 0]
    partner_ref[...] = rows_ref[:, place ^ 2, 0]
    for slot in range(slots):
        self_sum = neigh_sum = None
        for step, mean in enumerate((mean0, mean1, mean2, mean3)):
            part = place ^ step
            grad = rows_ref[:, part, 1, slot].reshape(segments * rows, columns).T
            layer_in = rows_ref[:, part, 0, slot].reshape(segments * rows, columns)
            self_term, neigh_term = matmul(grad, layer_in), matmul(grad, mean[slot])
            self_sum = self_term if self_sum is None else self_sum + self_term
            neigh_sum = neigh_term if neigh_sum is None else neigh_sum + neigh_term
        for kind, total in enumerate((self_sum, neigh_sum)):
            out_ref[:, kind, slot] = total.T.astype(BF16).reshape(shards, out_rows, columns)


def finish_kernel(half_ref, parts_ref, own_ref, missing_ref, self_ref, neigh_ref, out_ref):
    width = parts_ref.shape[5]
    for part in range(parts_ref.shape[0]):
        total = jnp.sum(parts_ref[part].astype(F32), axis=0)
        self_ref[:, :, part * width : (part + 1) * width] = total[0]
        neigh_ref[:, :, part * width : (part + 1) * width] = total[1]
    segments, slots, rows, columns = own_ref.shape
    for half in range(2):

        @pl.when(half_ref[0] == half)
        def _():
            for ref, at in ((own_ref, half), (missing_ref, 1 - half)):
                for slot in range(slots):
                    out_ref[slot, :, at * columns : (at + 1) * columns] = ref[:, slot].reshape(
                        segments * rows, columns
                    )


def round_y(block, step_of):
    size = lax.axis_size("segment")
    route = [(i, (i + 2 * step_of(i % 2)) % size) for i in range(size)]
    return lax.ppermute(block, "segment", route)


def core_swap(block):
    size = lax.axis_size("segment")
    return lax.ppermute(block, "segment", [(i, i ^ 1) for i in range(size)])


def x_swap(block, step):
    return lax.ppermute(block, ("xa", "xb"), [(i, i ^ step) for i in range(PAIR * PAIR)])


def exchange(block, axes):
    return lax.all_to_all(block, axes, split_axis=0, concat_axis=0, tiled=True)


def body(
    features,
    history,
    weight_self,
    weight_neigh,
    depth,
    send_index,
    pair_count,
    neighbours,
    cotangent,
):
    segments = lax.axis_size("segment")
    x_size = PAIR * PAIR
    z_size = lax.axis_size("z")
    shards = x_size * z_size
    my_segment = lax.axis_index("segment").reshape(1)
    my_half = lax.axis_index("xa").reshape(1)
    my_place = lax.axis_index(("xa", "xb")).reshape(1)
    my_shard = lax.axis_index(("xa", "xb", "z"))
    slots, nodes, width = history.shape
    rows_pair = send_index.shape[2]
    fanout = neighbours.shape[1]
    layers = segments * slots
    part = nodes // segments
    columns = width // 2
    received_rows = shards * rows_pair

    last_w = round_y(weight_self, lambda core: 1)
    next_w = round_y(weight_self, lambda core: -1)

    outgoing = pl.pallas_call(
        pick_kernel,
        out_shape=jax.ShapeDtypeStruct((shards, slots, rows_pair, width), BF16),
        compiler_params=params(12),
        name="pick_rows",
    )(send_index.reshape(received_rows, 1), history)
    received = exchange(outgoing, ("xa", "xb", "z"))

    last_w, next_w, other_w, token = lax.optimization_barrier(
        (last_w, next_w, core_swap(weight_self), depth.reshape(1, 1))
    )
    token = pl.pallas_call(
        token_kernel,
        out_shape=jax.ShapeDtypeStruct((1, 1), jnp.int32),
        in_specs=[pl.BlockSpec(memory_space=pltpu.SMEM)],
        out_specs=pl.BlockSpec(memory_space=pltpu.SMEM),
        cost_estimate=lasting(40),
        name="after_first_wave",
    )(token)
    my_counts = lax.dynamic_index_in_dim(pair_count, my_shard, 1, keepdims=True)
    live = (lax.iota(jnp.int32, rows_pair)[None, :] < my_counts).astype(F32)
    live = jnp.concatenate(
        [jnp.ones((1, nodes), F32), live.reshape(1, received_rows)], axis=1
    )
    smem = pl.BlockSpec(memory_space=pltpu.SMEM)
    vmem = pl.BlockSpec(memory_space=pltpu.VMEM)
    hbm = pl.BlockSpec(memory_space=pltpu.MemorySpace.HBM)
    counts_shape = (nodes, nodes + received_rows)
    counts = pl.pallas_call(
        count_kernel,
        out_specs=hbm,
        out_shape=jax.ShapeDtypeStruct(counts_shape, BF16),
        scratch_shapes=[pltpu.VMEM(counts_shape, BF16), pltpu.SemaphoreType.DMA],
        compiler_params=params(12),
        cost_estimate=lasting(2),
        name="count_rows",
    )(neighbours, live)

    _, last_w, next_w = lax.optimization_barrier((token, last_w, next_w))
    forwarded = jnp.where(lax.rem(my_segment[0], 2) == 0, last_w, next_w)
    far_w = round_y(forwarded, lambda core: 1 - 2 * core)
    next_other, last_other = core_swap(next_w), core_swap(last_w)

    term_rows = slots * part
    half_shape = jax.ShapeDtypeStruct((slots, nodes, columns), BF16)
    mean, others_mean, terms = pl.pallas_call(
        functools.partial(mean_kernel, fanout=fanout),
        in_specs=[smem, smem, hbm, hbm, hbm, hbm],
        out_specs=(hbm, hbm, hbm),
        scratch_shapes=[
            pltpu.VMEM(received.shape, BF16),
            pltpu.VMEM(counts_shape, BF16),
            pltpu.VMEM(history.shape, BF16),
            pltpu.VMEM(weight_neigh.shape, BF16),
            pltpu.VMEM(half_shape.shape, BF16),
            pltpu.VMEM(half_shape.shape, BF16),
            pltpu.VMEM((segments, term_rows, width), BF16),
            pltpu.SemaphoreType.DMA((7,)),
        ],
        out_shape=(
            half_shape,
            half_shape,
            jax.ShapeDtypeStruct((segments, term_rows, width), BF16),
        ),
        compiler_params=params(59.3),
        cost_estimate=lasting(2),
        name="neighbour_mean",
    )(depth, my_half, received, counts, history, weight_neigh)
    all_terms = exchange(terms, "segment")
    _, far_w, next_other, last_other = lax.optimization_barrier(
        (mean, far_w, next_other, last_other)
    )
    pieces = (
        weight_self, other_w, next_w, next_other, far_w, core_swap(far_w), last_w, last_other
    )

    anywhere = pl.BlockSpec(memory_space=pl.ANY)
    rows = pl.pallas_call(
        layers_kernel,
        in_specs=[smem, anywhere, anywhere, vmem] + [anywhere] * len(pieces),
        out_specs=anywhere,
        out_shape=jax.ShapeDtypeStruct((segments * x_size, 2, slots, part, columns), BF16),
        scratch_shapes=[
            pltpu.VMEM((segments * x_size, 2, slots, part, columns), BF16),
            pltpu.VMEM((part, width), BF16),
            pltpu.VMEM((part, width), BF16),
            pltpu.VMEM((layers, width, width), BF16),
            pltpu.VMEM((layers, part, width), F32),
            pltpu.VMEM((layers, part, width), F32),
            pltpu.SemaphoreType.DMA((segments,)),
            pltpu.SemaphoreType.DMA((segments,)),
        ],
        compiler_params=params(52),
        cost_estimate=lasting(13),
        name="all_layers",
    )(my_segment, features, cotangent, all_terms, *pieces)
    rows, *other_means = lax.optimization_barrier(
        (rows, x_swap(mean, 1), x_swap(others_mean, 2), x_swap(others_mean, 3))
    )
    means = (mean, *other_means)
    rows = exchange(rows, ("segment", "xa", "xb"))

    out_rows = width // shards
    sources = PAIR * z_size
    kept_shape = jax.ShapeDtypeStruct((segments, slots, part, columns), BF16)
    products, kept, for_partner = pl.pallas_call(
        product_kernel,
        in_specs=[smem] + [vmem] * 5,
        out_shape=(
            jax.ShapeDtypeStruct((sources, 2, slots, out_rows, columns), BF16),
            kept_shape,
            kept_shape,
        ),
        compiler_params=params(16),
        cost_estimate=lasting(3),
        name="weight_products",
    )(my_place, rows.reshape(segments, x_size, 2, slots, part, columns), *means)
    summands = exchange(products, ("xb", "z"))
    grad_shape = jax.ShapeDtypeStruct((slots, out_rows, width), F32)
    grad_self, grad_neigh, new_history = pl.pallas_call(
        finish_kernel,
        in_specs=[smem, vmem, vmem, vmem],
        out_shape=(grad_shape, grad_shape, jax.ShapeDtypeStruct((slots, nodes, width), BF16)),
        compiler_params=params(12),
        name="finish",
    )(
        my_half,
        summands.reshape(PAIR, z_size, 2, slots, out_rows, columns),
        kept,
        x_swap(for_partner, 2),
    )
    return (new_history, grad_self, grad_neigh)


def solution(mesh):
    segments, shards = mesh.devices.shape
    split = Mesh(
        mesh.devices.reshape(segments, PAIR, PAIR, shards // (PAIR * PAIR)),
        ("segment", "xa", "xb", "z"),
    )
    shard = ("xa", "xb", "z")
    return jax.shard_map(
        body,
        mesh=split,
        in_specs=(
            P(shard, None),
            P("segment", shard, None),
            P("segment", None, None),
            P("segment", None, None),
            P("segment"),
            P(shard, None, None),
            P(),
            P(shard, None),
            P(shard, None),
        ),
        out_specs=(
            P("segment", shard, None),
            P("segment", shard, None),
            P("segment", shard, None),
        ),
        check_vma=False,
    )
```
